256 devices in a mesh: expert: 8 (over y, core), dp: 32 (over x, z).
Axes of the slice: x: 4, y: 4, z: 8, core: 2. Of those that a mesh axis runs over, the one named last changes fastest.
Arguments:
- query_act: bfloat16 [512, 64, 1664], P('dp', 'expert'), may hold values from -5 to 5
- key_act: bfloat16 [512, 64, 1664], P('dp', 'expert'), may hold values from -5 to 5
- value_act: bfloat16 [512, 64, 1664], P('dp', 'expert'), may hold values from -6 to 6
- stream: bfloat16 [512, 64, 1664], P('dp', 'expert'), may hold values from -6 to 6
- grad_out: bfloat16 [512, 64, 1664], P('dp', 'expert'), may hold values from -6 to 6
- norm_gain: float32 [1664], replicated, may hold values from 0.25 to 1.75
- route_ids: int32 [32, 8, 128, 1], P('dp', 'expert'), may hold values from 0 to 31; in each aligned block of 128 rows (0 to 127, 128 to 255, ..., all dimensions but the last counted through in order) at most 6 rows name the same one
- gate_prob: float32 [32, 8, 128], P('dp', 'expert'), may hold values from 0.2 to 1
- weight_in: bfloat16 [32, 1664, 4096], P('dp', None, 'expert'), may hold values from -0.15625 to 0.15625
- weight_out: bfloat16 [32, 4096, 1664], P('dp', 'expert'), may hold values from -0.09375 to 0.09375
Outputs:
- grad_query: bfloat16 [512, 64, 1664], P('dp', 'expert')
- grad_key: bfloat16 [512, 64, 1664], P('dp', 'expert')
- grad_value: bfloat16 [512, 64, 1664], P('dp', 'expert')
- grad_stream: bfloat16 [512, 64, 1664], P('dp', 'expert')
- grad_weight_in: bfloat16 [32, 1664, 4096], P('dp', None, 'expert')
- grad_weight_out: bfloat16 [32, 4096, 1664], P('dp', 'expert')
The draws below stay inside these ranges and needn't reach their ends.
Inputs may be any that keep to these rules, and one draw needn't show every extreme that they name: `route_ids`: of the 128 patches of one device, at most 6 are routed to one expert, and some device sends exactly 6 to one expert.
All inputs are finite; a program needn't handle non-finite values.
Results may differ from the reference program's by a relative error of at most 0.024.
Values may be sent and summed in bfloat16 or wider, within the bound.
A program may use at most 128 MiB of HBM per device.

```python
import math
import jax
import jax.numpy as jnp
import numpy as np
from jax import lax

D = 1664
HEADS = 16
HD = 104
F = 4096
RAD = 6
IMW = 64
BAND = 16
COLS = 8
ROWS = 512
IMH = 512
TOK_DEV = 128
NTOK = 32768
EXPERTS = 32
CAP = 6
N_EXPERT = 8
N_DP = 32


def draw_query_act(key, part):
    key = jax.random.fold_in(key, 1)
    return jnp.clip(jax.random.normal(key, (ROWS, IMW, D)), -5.0, 5.0).astype(jnp.bfloat16)


def draw_key_act(key, part):
    key = jax.random.fold_in(key, 2)
    return jnp.clip(jax.random.normal(key, (ROWS, IMW, D)), -5.0, 5.0).astype(jnp.bfloat16)


def block_levels(own_key, dims, shards, smallest, high):
    gain, own = 1.0, jax.random.fold_in(own_key, 6)
    for axis_at, blocks in shards:
        heights = jnp.exp(jax.random.uniform(jax.random.fold_in(own, axis_at), (blocks,), jnp.float32, smallest / len(shards), high / len(shards)))
        gain = gain * jnp.repeat(heights, dims[axis_at] // blocks).reshape([-1 if axis == axis_at else 1 for axis in range(len(dims))])
    return gain


def assign_block(own_key, own, number, rows, count, top, most, slope):
    sequence = jax.random.permutation(own_key, count)
    packed, common = portions_of(count, rows * top, most, slope, True), portions_of(count, rows * top, most, slope, False)
    places = jnp.arange(count)

    def named(lengths, turn):
        used = int((lengths > 0).sum())
        fixed = max(1, used // 4)
        moved = fixed + (places - fixed + turn * (used - fixed)) % max(1, count - fixed)
        return jnp.zeros((count,), jnp.int32).at[sequence[jnp.where(places < fixed, places, moved)]].set(jnp.asarray(lengths, jnp.int32))

    lengths = jnp.where(number % 4 == 0, named(packed, number // 4), named(common, number - number // 4 - 1))
    mixed = jax.random.permutation(jax.random.fold_in(own, 3), count)
    giver, taker = mixed[0:count // 2 * 2:2], mixed[1:count // 2 * 2:2]
    slack = jnp.minimum(lengths[giver] - 1, most - lengths[taker]) // 2
    slack = jnp.where((giver == sequence[0]) | (taker == sequence[0]) | (lengths[taker] == 0), 0, jnp.maximum(slack, 0))
    moved = jax.random.randint(jax.random.fold_in(own, 4), (count // 2,), 0, 1 << 20) % (slack + 1)
    lengths = lengths.at[giver].add(-moved).at[taker].add(moved)
    members = jnp.searchsorted(jnp.cumsum(lengths), jnp.arange(rows * top), side="right").astype(jnp.int32)
    table = members.reshape(top, rows).T
    table = table[jax.random.permutation(jax.random.fold_in(own, 1), rows)]
    turn = jax.random.randint(jax.random.fold_in(own, 2), (rows, 1), 0, top)
    return jnp.take_along_axis(table, (jnp.arange(top)[None, :] + turn) % top, axis=1)


def portions_of(number_of, total, reach, skew, full):
    weights = [(1 << 20) // math.isqrt(standing ** skew) + 1 for standing in range(1, number_of + 1)]
    largest = reach if full else min(reach, max(-(-total // number_of), total * weights[0] // sum(weights)))
    least = 1 if total - largest >= number_of - 1 else 0
    given, surplus = [largest] + [least] * (number_of - 1), total - largest - least * (number_of - 1)
    while surplus > 0:
        free = [i for i in range(1, number_of) if given[i] < largest] or [i for i in range(1, number_of) if given[i] < reach]
        pool, remaining = sum([weights[i] for i in free]), surplus
        for i in free:
            extra = min(reach - given[i], max(1, remaining * weights[i] // pool), surplus)
            given[i] = given[i] + extra
            surplus = surplus - extra
    return np.array(given)


def noise(rng, shape, width, reach, shards=(), held_as=jnp.bfloat16):
    result = jax.random.normal(rng, shape, jnp.float32) * width
    if len(shards) > 0:
        result = block_levels(rng, shape, shards, -0.22, 0.18) * result
    return jnp.clip(result, min=-reach, max=reach).astype(held_as)


def setup_inputs(seed: int = 0) -> dict:
    keys = jax.random.split(jax.random.key(seed), 11)
    query_act = draw_query_act(jax.random.fold_in(keys[10], 71), 0)
    key_act = draw_key_act(jax.random.fold_in(keys[10], 71), 0)
    value_act = noise(keys[2], (ROWS, IMW, D), 1.0, 6.0, ((0, 32), (1, 8)))
    stream = noise(keys[3], (ROWS, IMW, D), 1.0, 6.0, ((0, 32), (1, 8)))
    grad_out = noise(keys[4], (ROWS, IMW, D), 1.0, 6.0, ((0, 32), (1, 8)))
    norm_gain = jnp.clip(1.0 + 0.15 * jax.random.normal(keys[5], (D,), jnp.float32), 0.25, 1.75)
    route_ids_keys = jax.random.split(jax.random.fold_in(keys[6], 1), N_DP * N_EXPERT * TOK_DEV // TOK_DEV)
    route_ids_turns = jax.random.permutation(jax.random.fold_in(keys[6], 3), N_DP * N_EXPERT * TOK_DEV // TOK_DEV)
    route_ids = jax.vmap(lambda own, number: assign_block(jax.random.fold_in(keys[6], 2), own, number, TOK_DEV, EXPERTS, 1, CAP, 2))(route_ids_keys, route_ids_turns).reshape((N_DP, N_EXPERT, TOK_DEV, 1))
    gate_prob = jnp.clip(jnp.exp(math.log(1.0) - 1.609438 * jax.random.uniform(keys[7], (N_DP, N_EXPERT, TOK_DEV), jnp.float32) ** block_levels(keys[7], (N_DP, N_EXPERT, TOK_DEV), ((0, 32), (1, 8)), -0.2, 0.2)), 0.2, 1.0)
    weight_in = noise(keys[8], (EXPERTS, D, F), D ** -0.5, 0.15625, ((0, 32), (2, 8)))
    weight_out = noise(keys[9], (EXPERTS, F, D), F ** -0.5, 0.09375, ((0, 32), (1, 8)))
    return {"query_act": query_act, "key_act": key_act, "value_act": value_act, "stream": stream, "grad_out": grad_out, "norm_gain": norm_gain, "route_ids": route_ids, "gate_prob": gate_prob, "weight_in": weight_in, "weight_out": weight_out}


LN_EPS = 1e-05
ROOT_HALF = 0.7071067811865476
INV_ROOT_TAU = 0.3989422804014327
NEG_LARGE = -1e+30

def gelu_value(values):
    return 0.5 * values * (1.0 + lax.erf(values * ROOT_HALF))

def gelu_slope(values):
    return 0.5 * (1.0 + lax.erf(values * ROOT_HALF)) + values * jnp.exp(-0.5 * values * values) * INV_ROOT_TAU

def layer_norm(stream, norm_gain):
    values = stream.astype(jnp.float32)
    center = values - lax.optimization_barrier(jnp.mean(values, axis=-1, keepdims=True))
    inv_std = lax.rsqrt(lax.optimization_barrier(jnp.mean(center * center, axis=-1, keepdims=True)) + LN_EPS)
    normed = center * inv_std
    return (normed, inv_std, (normed * norm_gain).astype(jnp.bfloat16))

def norm_backward(grad_in, normed, inv_std, norm_gain):
    scaled = grad_in.astype(jnp.float32) * norm_gain
    centered = scaled - lax.optimization_barrier(jnp.mean(scaled, axis=-1, keepdims=True))
    return inv_std * (centered - normed * lax.optimization_barrier(jnp.mean(scaled * normed, axis=-1, keepdims=True)))

def expert_grads(rows_in, rows_grad, w_first, w_second):
    pre_act = jnp.dot(rows_in, w_first, preferred_element_type=jnp.float32)
    hidden = gelu_value(pre_act).astype(jnp.bfloat16)
    grad_hidden = lax.dot_general(rows_grad, w_second, (((1,), (1,)), ((), ())), preferred_element_type=jnp.float32)
    grad_pre = (grad_hidden * gelu_slope(pre_act)).astype(jnp.bfloat16)
    grad_second = lax.dot_general(hidden, rows_grad, (((0,), (0,)), ((), ())), preferred_element_type=jnp.float32)
    grad_first = lax.dot_general(rows_in, grad_pre, (((0,), (0,)), ((), ())), preferred_element_type=jnp.float32)
    back_terms = lax.dot_general(grad_pre, w_first, (((1,), (1,)), ((), ())), preferred_element_type=jnp.float32)
    return (grad_first.astype(jnp.bfloat16), grad_second.astype(jnp.bfloat16), back_terms)

def to_blocks(array):
    return array.reshape(N_DP, BAND, N_EXPERT, COLS, D).transpose(0, 2, 1, 3, 4).reshape(NTOK, D)

def from_blocks(array):
    return array.reshape(N_DP, N_EXPERT, BAND, COLS, D).transpose(0, 2, 1, 3, 4).reshape(ROWS, IMW, D)

def reference(query_act, key_act, value_act, stream, grad_out, norm_gain, route_ids, gate_prob, weight_in, weight_out):
    devices_total = N_DP * N_EXPERT
    flat_stream = to_blocks(stream)
    flat_grad = to_blocks(grad_out)
    normed, inv_std, expert_in = layer_norm(flat_stream, norm_gain)
    grad_z = (gate_prob.reshape(NTOK, 1) * flat_grad.astype(jnp.float32)).astype(jnp.bfloat16)
    routes = route_ids.reshape(devices_total, TOK_DEV).astype(jnp.int32)
    onehot = (routes[:, :, None] == jnp.arange(EXPERTS, dtype=jnp.int32)[None, None, :]).astype(jnp.int32)
    ranks = lax.optimization_barrier(jnp.sum((jnp.cumsum(onehot, axis=1) - onehot) * onehot, axis=2)).astype(jnp.int32)
    position = (jnp.arange(devices_total, dtype=jnp.int32)[:, None] * CAP + ranks).reshape(NTOK).astype(jnp.int32)
    experts_of = routes.reshape(NTOK)
    buffer_in = jnp.zeros((EXPERTS, devices_total * CAP, D), jnp.bfloat16).at[experts_of, position].set(expert_in)
    buffer_grad = jnp.zeros((EXPERTS, devices_total * CAP, D), jnp.bfloat16).at[experts_of, position].set(grad_z)

    def per_expert(operands):
        w_first, w_second, rows_in, rows_grad = operands
        grad_first, grad_second, back_terms = expert_grads(rows_in, rows_grad, w_first, w_second)
        return (grad_first, grad_second, back_terms.astype(jnp.bfloat16))
    grad_weight_in, grad_weight_out, back_rows = lax.map(per_expert, (weight_in, weight_out, buffer_in, buffer_grad))
    grad_u = back_rows[experts_of, position].astype(jnp.float32)
    grad_flat = (flat_grad.astype(jnp.float32) + norm_backward(grad_u, normed, inv_std, norm_gain)).astype(jnp.bfloat16)
    grad_stream = from_blocks(grad_flat)
    span = 2 * RAD + 1
    scale = HD ** (-0.5)
    zero_index = jnp.zeros((), jnp.int32)
    pad_widths = ((RAD, RAD), (RAD, RAD), (0, 0), (0, 0))
    query_f = query_act.reshape(ROWS, IMW, HEADS, HD).astype(jnp.float32)
    keys_pad = jnp.pad(key_act.reshape(ROWS, IMW, HEADS, HD), pad_widths)
    values_pad = jnp.pad(value_act.reshape(ROWS, IMW, HEADS, HD), pad_widths)
    grad_heads = grad_stream.reshape(ROWS, IMW, HEADS, HD).astype(jnp.float32)
    row_ids = jnp.arange(ROWS, dtype=jnp.int32)
    col_ids = jnp.arange(IMW, dtype=jnp.int32)
    offsets = jnp.arange(span * span, dtype=jnp.int32)

    def start_of(offset):
        offset = offset.astype(jnp.int32)
        return (offset // span, offset % span, zero_index, zero_index)

    def shifted(array, offset):
        return lax.dynamic_slice(array, start_of(offset), (ROWS, IMW, HEADS, HD)).astype(jnp.float32)

    def valid_at(offset):
        key_row = row_ids + offset // span - RAD
        key_col = col_ids + offset % span - RAD
        row_fine = (key_row >= 0) & (key_row < ROWS) & (key_row // IMH == row_ids // IMH)
        col_fine = (key_col >= 0) & (key_col < IMW)
        return row_fine[:, None] & col_fine[None, :]

    def score_at(offset):
        scores = lax.optimization_barrier(jnp.sum(query_f * shifted(keys_pad, offset), axis=-1)) * scale
        return jnp.where(valid_at(offset)[:, :, None], scores, NEG_LARGE)
    masked = lax.map(score_at, offsets)
    peak = lax.optimization_barrier(jnp.max(masked, axis=0))
    log_total = peak + jnp.log(lax.optimization_barrier(jnp.sum(jnp.exp(masked - peak), axis=0)))
    probs = jnp.exp(masked - log_total)
    probs_low = lax.optimization_barrier(probs.astype(jnp.bfloat16)).astype(jnp.float32)

    def add_values(offset, carry):
        return carry + probs_low[offset][..., None] * shifted(values_pad, offset)
    attended = lax.fori_loop(0, span * span, add_values, jnp.zeros((ROWS, IMW, HEADS, HD), jnp.float32))
    delta = lax.optimization_barrier(jnp.sum(grad_heads * attended, axis=-1))

    def grad_prob_at(offset):
        return lax.optimization_barrier(jnp.sum(grad_heads * shifted(values_pad, offset), axis=-1))
    grad_probs = lax.map(grad_prob_at, offsets)
    grad_scores = lax.optimization_barrier((probs * (grad_probs - delta)).astype(jnp.bfloat16)).astype(jnp.float32)

    def add_query(offset, carry):
        return carry + grad_scores[offset][..., None] * shifted(keys_pad, offset)
    grad_query = lax.fori_loop(0, span * span, add_query, jnp.zeros((ROWS, IMW, HEADS, HD), jnp.float32)) * scale

    def spread_back(offset, carry):
        key_acc, value_acc = carry
        start = start_of(offset)
        shape = (ROWS, IMW, HEADS, HD)
        key_acc = lax.dynamic_update_slice(key_acc, lax.dynamic_slice(key_acc, start, shape) + grad_scores[offset][..., None] * query_f, start)
        value_acc = lax.dynamic_update_slice(value_acc, lax.dynamic_slice(value_acc, start, shape) + probs_low[offset][..., None] * grad_heads, start)
        return (key_acc, value_acc)
    empty = jnp.zeros((ROWS + 2 * RAD, IMW + 2 * RAD, HEADS, HD), jnp.float32)
    key_acc, value_acc = lax.fori_loop(0, span * span, spread_back, (empty, empty))
    grad_key = key_acc[RAD:RAD + ROWS, RAD:RAD + IMW] * scale
    grad_value = value_acc[RAD:RAD + ROWS, RAD:RAD + IMW]
    return (grad_query.reshape(ROWS, IMW, D).astype(jnp.bfloat16), grad_key.reshape(ROWS, IMW, D).astype(jnp.bfloat16), grad_value.reshape(ROWS, IMW, D).astype(jnp.bfloat16), grad_stream, grad_weight_in, grad_weight_out)
```

```python
import functools

import jax
import jax.numpy as jnp
from jax import lax
from jax.experimental import pallas as pl
from jax.experimental.pallas import tpu as pltpu
from jax.sharding import PartitionSpec as P

HEADS = 16
RAD = 6
VMEM_LIMIT = 48 * 1024 * 1024


LN_EPS = 1e-05
ROOT_HALF = 0.7071067811865476
INV_ROOT_TAU = 0.3989422804014327
NEG_LARGE = -1e30


def gelu_value(values):
    return 0.5 * values * (1.0 + lax.erf(values * ROOT_HALF))


def gelu_slope(values):
    return (
        0.5 * (1.0 + lax.erf(values * ROOT_HALF))
        + values * jnp.exp(-0.5 * values * values) * INV_ROOT_TAU
    )


def layer_norm(stream, norm_gain):
    values = stream.astype(jnp.float32)
    center = values - jnp.mean(values, axis=-1, keepdims=True)
    inv_std = lax.rsqrt(jnp.mean(center * center, axis=-1, keepdims=True) + LN_EPS)
    normed = center * inv_std
    return (normed, inv_std, (normed * norm_gain).astype(jnp.bfloat16))


def norm_backward(grad_in, normed, inv_std, norm_gain):
    scaled = grad_in * norm_gain
    centered = scaled - jnp.mean(scaled, axis=-1, keepdims=True)
    return inv_std * (centered - normed * jnp.mean(scaled * normed, axis=-1, keepdims=True))


def expert_grads(rows_in, rows_grad, w_first, w_second):
    pre_act = jnp.dot(rows_in, w_first, preferred_element_type=jnp.float32)
    hidden = gelu_value(pre_act).astype(jnp.bfloat16)
    grad_hidden = lax.dot_general(
        rows_grad, w_second, (((1,), (1,)), ((), ())), preferred_element_type=jnp.float32
    )
    grad_pre = (grad_hidden * gelu_slope(pre_act)).astype(jnp.bfloat16)
    grad_second = lax.dot_general(
        hidden, rows_grad, (((0,), (0,)), ((), ())), preferred_element_type=jnp.float32
    )
    grad_first = lax.dot_general(
        rows_in, grad_pre, (((0,), (0,)), ((), ())), preferred_element_type=jnp.float32
    )
    back_terms = lax.dot_general(
        grad_pre, w_first, (((1,), (1,)), ((), ())), preferred_element_type=jnp.float32
    )
    return (grad_first.astype(jnp.bfloat16), grad_second.astype(jnp.bfloat16), back_terms)


def dispatch_table(routes, experts, capacity):
    tokens = routes.shape[0]
    onehot = (routes[:, None] == jnp.arange(experts, dtype=jnp.int32)[None, :]).astype(jnp.bfloat16)
    earlier = (jnp.arange(tokens)[:, None] > jnp.arange(tokens)[None, :]).astype(jnp.bfloat16)
    before = jnp.dot(earlier, onehot, preferred_element_type=jnp.float32)
    ranks = jnp.sum(before * onehot.astype(jnp.float32), axis=1).astype(jnp.int32)
    target = routes * capacity + ranks
    return (jnp.arange(experts * capacity, dtype=jnp.int32)[:, None] == target[None, :]).astype(
        jnp.bfloat16
    )


def head_lanes(head, size, width):
    start = head * size
    low = start // 128 * 128
    high = min((start + size + 127) // 128 * 128, width)
    return start, low, high


def lane_mask(head, size, low, high):
    lanes = lax.broadcasted_iota(jnp.int32, (1, high - low), 1) + low
    return (lanes >= head * size) & (lanes < (head + 1) * size)


def nt_dot(left, right):
    return lax.dot_general(left, right, (((1,), (1,)), ((), ())), preferred_element_type=jnp.float32)


def nn_dot(left, right):
    return jnp.dot(left, right, preferred_element_type=jnp.float32)


def window_bias(band, cols, rows_total, cols_total):
    row_index = lax.axis_index("dp")
    col_index = lax.axis_index("expert")
    side = (band + 2 * RAD) * cols
    shape = (band * cols, 3 * side)
    shift = cols.bit_length() - 1
    own = lax.broadcasted_iota(jnp.int32, shape, 0)
    far = lax.broadcasted_iota(jnp.int32, shape, 1)
    part = (far >= side).astype(jnp.int32) + (far >= 2 * side).astype(jnp.int32)
    within = far - side * part
    far_row = (within >> shift) - RAD
    far_col = (within & (cols - 1)) + cols * (part - 1)
    own_row = own >> shift
    own_col = own & (cols - 1)
    abs_row = far_row + row_index * band
    abs_col = far_col + col_index * cols
    fine = (
        (jnp.abs(far_row - own_row) <= RAD)
        & (jnp.abs(far_col - own_col) <= RAD)
        & (abs_row >= 0)
        & (abs_row < rows_total)
        & (abs_col >= 0)
        & (abs_col < cols_total)
    )
    return jnp.where(fine, 0.0, NEG_LARGE)


def tall(refs, low, high):
    return jnp.concatenate([ref[:, low:high] for ref in refs], axis=0)


def forward_kernel(sizes, query_ref, left_ref, mid_ref, right_ref, att_ref, stats_ref, bias_ref):
    band, cols, rows_total, cols_total = sizes
    width = query_ref.shape[1]
    size = width // HEADS
    scale = size ** (-0.5)
    refs = (left_ref, mid_ref, right_ref)
    bias_ref[...] = window_bias(band, cols, rows_total, cols_total)
    att_ref[...] = jnp.zeros_like(att_ref)
    lanes = lax.broadcasted_iota(jnp.int32, stats_ref.shape, 1)
    stats = jnp.zeros(stats_ref.shape, jnp.float32)
    for head in range(HEADS):
        start, low, high = head_lanes(head, size, width)
        mask = lane_mask(head, size, low, high)
        queries = query_ref[:, low:high] * mask.astype(jnp.bfloat16)
        scores = nt_dot(queries, tall(refs, low, high)) * scale + bias_ref[...]
        peak = jnp.max(scores, axis=-1, keepdims=True)
        log_total = peak + jnp.log(jnp.sum(jnp.exp(scores - peak), axis=-1, keepdims=True))
        probs_low = jnp.exp(scores - log_total).astype(jnp.bfloat16)
        attended = nn_dot(probs_low, tall(refs, width + low, width + high))
        att_ref[:, low:high] += jnp.where(mask, attended, 0.0)
        stats = jnp.where(lanes == head, log_total, stats)
    stats_ref[...] = stats


def split_three(values):
    first = values.astype(jnp.bfloat16)
    rest = values - first.astype(jnp.float32)
    second = rest.astype(jnp.bfloat16)
    third = (rest - second.astype(jnp.float32)).astype(jnp.bfloat16)
    return first, second, third


def stream_kernel(stream_ref, grad_ref, gain_ref, back_ref, att_ref, stats_ref, plain_ref, packed_ref):
    width = stream_ref.shape[1]
    size = width // HEADS
    gain = gain_ref[...]
    normed, inv_std, _ = layer_norm(stream_ref[...], gain)
    grad_stream = (
        grad_ref[...].astype(jnp.float32) + norm_backward(back_ref[...], normed, inv_std, gain)
    ).astype(jnp.bfloat16)
    plain_ref[...] = grad_stream
    packed_ref[:, :width] = grad_stream
    products = grad_stream.astype(jnp.float32) * att_ref[...]
    feature = lax.broadcasted_iota(jnp.int32, (width, 128), 0)
    first = lax.broadcasted_iota(jnp.int32, (width, 128), 1) * size
    owner = jnp.where((feature >= first) & (feature < first + size), 1.0, 0.0).astype(jnp.bfloat16)
    delta = sum(nn_dot(piece, owner) for piece in split_three(products))
    source = lax.broadcasted_iota(jnp.int32, (128, 128), 0)
    target = lax.broadcasted_iota(jnp.int32, (128, 128), 1)
    total = jnp.zeros(delta.shape, jnp.float32)
    pieces = split_three(stats_ref[...]) + split_three(delta)
    for place, piece in enumerate(pieces):
        move = (target == source + place * HEADS) & (source < HEADS)
        total = total + nn_dot(piece, jnp.where(move, 1.0, 0.0).astype(jnp.bfloat16))
    packed_ref[:, width:] = total.astype(jnp.bfloat16)


def backward_kernel(
    sizes,
    left_ref,
    mid_ref,
    right_ref,
    gleft_ref,
    gmid_ref,
    gright_ref,
    gq_ref,
    gk_ref,
    gv_ref,
    bias_ref,
    acc_q,
    acc_k,
    acc_v,
):
    band, cols, rows_total, cols_total = sizes
    width = gq_ref.shape[1]
    size = width // HEADS
    scale = size ** (-0.5)
    tokens = band * cols
    own = slice(RAD * cols, RAD * cols + tokens)
    refs = (left_ref, mid_ref, right_ref)
    grefs = (gleft_ref, gmid_ref, gright_ref)
    bias_ref[...] = window_bias(band, cols, rows_total, cols_total)
    for acc in (acc_q, acc_k, acc_v):
        acc[...] = jnp.zeros_like(acc)
    row = lax.broadcasted_iota(jnp.int32, (2 * HEADS, 128), 0)
    lane = lax.broadcasted_iota(jnp.int32, (2 * HEADS, 128), 1)
    base = jnp.where(row < HEADS, row, row + 2 * HEADS)
    pick = jnp.where(
        (lane == base) | (lane == base + HEADS) | (lane == base + 2 * HEADS), 1.0, 0.0
    ).astype(jnp.bfloat16)
    stats_far = nt_dot(pick, tall(grefs, width, width + 128))
    stats_own = nt_dot(gmid_ref[own, width : width + 128], pick)
    for head in range(HEADS):
        start, low, high = head_lanes(head, size, width)
        mask = lane_mask(head, size, low, high)
        mask_low = mask.astype(jnp.bfloat16)
        keys = tall(refs, low, high)
        values = tall(refs, width + low, width + high)
        queries = tall(refs, 2 * width + low, 2 * width + high)
        grads = tall(grefs, low, high)
        bias = bias_ref[...]
        own_key = mid_ref[own, low:high] * mask_low
        own_value = mid_ref[own, width + low : width + high] * mask_low
        own_query = mid_ref[own, 2 * width + low : 2 * width + high] * mask_low
        own_grad = gmid_ref[own, low:high] * mask_low

        probs = jnp.exp(
            nt_dot(own_query, keys) * scale + bias - stats_own[:, head : head + 1]
        )
        grad_probs = nt_dot(own_grad, values)
        grad_scores = (
            probs * (grad_probs - stats_own[:, HEADS + head : HEADS + head + 1])
        ).astype(jnp.bfloat16)
        acc_q[:, low:high] += jnp.where(mask, nn_dot(grad_scores, keys), 0.0)

        probs = jnp.exp(
            nt_dot(own_key, queries) * scale + bias - stats_far[head : head + 1, :]
        )
        acc_v[:, low:high] += jnp.where(mask, nn_dot(probs.astype(jnp.bfloat16), grads), 0.0)
        grad_probs = nt_dot(own_value, grads)
        grad_scores = (
            probs * (grad_probs - stats_far[HEADS + head : HEADS + head + 1, :])
        ).astype(jnp.bfloat16)
        acc_k[:, low:high] += jnp.where(mask, nn_dot(grad_scores, queries), 0.0)
    gq_ref[...] = (acc_q[...] * scale).astype(jnp.bfloat16)
    gk_ref[...] = (acc_k[...] * scale).astype(jnp.bfloat16)
    gv_ref[...] = acc_v[...].astype(jnp.bfloat16)


def vmem():
    return pl.BlockSpec(memory_space=pltpu.VMEM)


def wide_halo(block, rim):
    def pairs(axis):
        count = lax.axis_size(axis)
        forward = [(i, i + 1) for i in range(count - 1)]
        return forward, [(b, a) for a, b in forward]

    forward, backward = pairs("dp")
    upper = lax.ppermute(block[block.shape[0] - rim :], "dp", forward)
    lower = lax.ppermute(block[:rim], "dp", backward)
    mid = jnp.concatenate([upper, block, lower], axis=0)
    forward, backward = pairs("expert")
    left = lax.ppermute(mid, "expert", forward)
    right = lax.ppermute(mid, "expert", backward)
    return left, mid, right

def body(
    query_act,
    key_act,
    value_act,
    stream,
    grad_out,
    norm_gain,
    route_ids,
    gate_prob,
    weight_in,
    weight_out,
):
    band, cols, width = stream.shape
    tokens = band * cols
    experts = lax.axis_size("dp")
    col_parts = lax.axis_size("expert")
    capacity = max(2, tokens * 3 // (2 * experts))
    sizes = (band, cols, band * experts, cols * col_parts)
    side = (band + 2 * RAD) * cols
    flat_query = query_act.reshape(tokens, width)
    joined = jnp.concatenate(
        [key_act.reshape(tokens, width), value_act.reshape(tokens, width), flat_query], axis=-1
    )
    near = wide_halo(joined, RAD * cols)
    attended, log_total = pl.pallas_call(
        functools.partial(forward_kernel, sizes),
        out_shape=(
            jax.ShapeDtypeStruct((tokens, width), jnp.float32),
            jax.ShapeDtypeStruct((tokens, 128), jnp.float32),
        ),
        in_specs=[vmem()] * 4,
        out_specs=(vmem(), vmem()),
        scratch_shapes=[pltpu.VMEM((tokens, 3 * side), jnp.float32)],
        compiler_params=pltpu.CompilerParams(vmem_limit_bytes=VMEM_LIMIT),
        name="attend",
    )(flat_query, *near)
    flat_stream = stream.reshape(tokens, width)
    flat_grad = grad_out.reshape(tokens, width)
    normed, inv_std, expert_in = layer_norm(flat_stream, norm_gain)
    grad_z = (gate_prob.reshape(tokens, 1) * flat_grad.astype(jnp.float32)).astype(jnp.bfloat16)
    table = dispatch_table(route_ids.reshape(tokens), experts, capacity)
    slots_in = (
        jnp.dot(table, expert_in, preferred_element_type=jnp.float32)
        .astype(jnp.bfloat16)
        .reshape(experts, capacity, width)
    )
    slots_grad = (
        jnp.dot(table, grad_z, preferred_element_type=jnp.float32)
        .astype(jnp.bfloat16)
        .reshape(experts, capacity, width)
    )
    arrived_in, arrived_grad = (
        lax.all_to_all(slots_in, "dp", split_axis=0, concat_axis=0, tiled=True),
        lax.all_to_all(slots_grad, "dp", split_axis=0, concat_axis=0, tiled=True),
    )
    rows_in, rows_grad = (
        lax.all_gather(arrived_in, "expert", axis=0, tiled=True),
        lax.all_gather(arrived_grad, "expert", axis=0, tiled=True),
    )
    grad_first, grad_second, back_terms = expert_grads(
        rows_in.reshape(-1, width), rows_grad.reshape(-1, width), weight_in[0], weight_out[0]
    )
    own_terms = lax.psum_scatter(
        back_terms.reshape(col_parts, experts * capacity, width).astype(jnp.bfloat16),
        "expert",
        scatter_dimension=0,
        tiled=True,
    )
    returned = lax.all_to_all(
        own_terms.reshape(experts, capacity, width), "dp", split_axis=0, concat_axis=0, tiled=True
    )
    grad_u = lax.dot_general(
        table,
        returned.reshape(experts * capacity, width),
        (((0,), (0,)), ((), ())),
        preferred_element_type=jnp.float32,
    )
    plain, packed = pl.pallas_call(
        stream_kernel,
        out_shape=(
            jax.ShapeDtypeStruct((tokens, width), jnp.bfloat16),
            jax.ShapeDtypeStruct((tokens, width + 128), jnp.bfloat16),
        ),
        in_specs=[vmem()] * 6,
        out_specs=(vmem(), vmem()),
        compiler_params=pltpu.CompilerParams(vmem_limit_bytes=VMEM_LIMIT),
        name="stream_grad",
    )(flat_stream, flat_grad, norm_gain.reshape(1, width), grad_u, attended, log_total)
    far = wide_halo(packed, RAD * cols)
    grad_query, grad_key, grad_value = pl.pallas_call(
        functools.partial(backward_kernel, sizes),
        out_shape=(jax.ShapeDtypeStruct((tokens, width), jnp.bfloat16),) * 3,
        in_specs=[vmem()] * 6,
        out_specs=(vmem(),) * 3,
        scratch_shapes=[pltpu.VMEM((tokens, 3 * side), jnp.float32)]
        + [pltpu.VMEM((tokens, width), jnp.float32)] * 3,
        compiler_params=pltpu.CompilerParams(vmem_limit_bytes=VMEM_LIMIT),
        name="attend_back",
    )(*near, *far)
    shape = (band, cols, width)
    return (
        grad_query.reshape(shape),
        grad_key.reshape(shape),
        grad_value.reshape(shape),
        plain.reshape(shape),
        grad_first[None],
        grad_second[None],
    )


def solution(mesh):
    in_specs = (
        P("dp", "expert", None),
        P("dp", "expert", None),
        P("dp", "expert", None),
        P("dp", "expert", None),
        P("dp", "expert", None),
        P(),
        P("dp", "expert", None, None),
        P("dp", "expert", None),
        P("dp", None, "expert"),
        P("dp", "expert", None),
    )
    out_specs = (
        P("dp", "expert", None),
        P("dp", "expert", None),
        P("dp", "expert", None),
        P("dp", "expert", None),
        P("dp", None, "expert"),
        P("dp", "expert", None),
    )
    return jax.shard_map(body, mesh=mesh, in_specs=in_specs, out_specs=out_specs, check_vma=False)
```

```python
import functools

import jax
import jax.numpy as jnp
from jax import lax
from jax.experimental import pallas as pl
from jax.experimental.pallas import tpu as pltpu
from jax.sharding import PartitionSpec as P

HEADS = 16
RAD = 6
SLOTS = 6
MESH = pl.DeviceIdType.MESH
VMEM_LIMIT = 48 * 1024 * 1024


LN_EPS = 1e-05
ROOT_HALF = 0.7071067811865476
INV_ROOT_TAU = 0.3989422804014327
NEG_LARGE = -1e30


def gelu_value(values):
    return 0.5 * values * (1.0 + lax.erf(values * ROOT_HALF))


def gelu_slope(values):
    return (
        0.5 * (1.0 + lax.erf(values * ROOT_HALF))
        + values * jnp.exp(-0.5 * values * values) * INV_ROOT_TAU
    )


def layer_norm(stream, norm_gain):
    values = stream.astype(jnp.float32)
    center = values - jnp.mean(values, axis=-1, keepdims=True)
    inv_std = lax.rsqrt(jnp.mean(center * center, axis=-1, keepdims=True) + LN_EPS)
    normed = center * inv_std
    return (normed, inv_std, (normed * norm_gain).astype(jnp.bfloat16))


def norm_backward(grad_in, normed, inv_std, norm_gain):
    scaled = grad_in * norm_gain
    centered = scaled - jnp.mean(scaled, axis=-1, keepdims=True)
    return inv_std * (centered - normed * jnp.mean(scaled * normed, axis=-1, keepdims=True))


def expert_grads(rows_in, rows_grad, w_first, w_second):
    pre_act = jnp.dot(rows_in, w_first, preferred_element_type=jnp.float32)
    hidden = gelu_value(pre_act).astype(jnp.bfloat16)
    grad_hidden = lax.dot_general(
        rows_grad, w_second, (((1,), (1,)), ((), ())), preferred_element_type=jnp.float32
    )
    grad_pre = (grad_hidden * gelu_slope(pre_act)).astype(jnp.bfloat16)
    grad_second = lax.dot_general(
        hidden, rows_grad, (((0,), (0,)), ((), ())), preferred_element_type=jnp.float32
    )
    grad_first = lax.dot_general(
        rows_in, grad_pre, (((0,), (0,)), ((), ())), preferred_element_type=jnp.float32
    )
    back_terms = lax.dot_general(
        grad_pre, w_first, (((1,), (1,)), ((), ())), preferred_element_type=jnp.float32
    )
    return (grad_first.astype(jnp.bfloat16), grad_second.astype(jnp.bfloat16), back_terms)


def unit_places(index, first):
    place = index % 16
    block = index // 16
    rank = place - first
    return jnp.where((rank >= 0) & (rank < SLOTS), block * SLOTS + rank, -1)


def slot_rows(index):
    place = index % 16
    block = index // 16
    tail = jnp.where(place >= 12, block * SLOTS + place - 12, -1)
    late = jnp.where((place == 12) | (place == 13), block * SLOTS + place - 8, -1)
    last = jnp.where(place >= 14, block * SLOTS + place - 10, -1)
    return (unit_places(index, 0), unit_places(index, 6), tail, late, last)


def pack_tables(slots, rows):
    index = lax.broadcasted_iota(jnp.int32, (rows, 1), 0)
    return [jnp.where(held == slots, 1.0, 0.0).astype(jnp.bfloat16) for held in slot_rows(index)]


def unpack_tables(slots, rows):
    index = lax.broadcasted_iota(jnp.int32, (1, rows), 1)
    return [jnp.where(held == slots, 1.0, 0.0).astype(jnp.bfloat16) for held in slot_rows(index)]


def pack_rows(tables, values):
    t0, t1, t2, t3, t4 = tables
    chunk = [values[:, 128 * i : 128 * (i + 1)] for i in range(10, 13)]
    tail = jnp.concatenate(
        [
            nn_dot(t2, values[:, 1280:1664]),
            nn_dot(t3, chunk[0]) + nn_dot(t4, chunk[1]),
            nn_dot(t3, chunk[2]),
        ],
        axis=1,
    )
    return (nn_dot(t0, values[:, :640]) + nn_dot(t1, values[:, 640:1280]) + tail).astype(
        jnp.bfloat16
    )


def unpack_rows(tables, packed):
    t0, t1, t2, t3, t4 = tables
    third, fourth = packed[:, 384:512], packed[:, 512:640]
    extra = jnp.concatenate([nn_dot(t3, third), nn_dot(t4, third), nn_dot(t3, fourth)], axis=1)
    return jnp.concatenate(
        [nn_dot(t0, packed), nn_dot(t1, packed), nn_dot(t2, packed[:, :384]) + extra], axis=1
    )


def as_column(row):
    count = row.shape[1]
    diagonal = lax.broadcasted_iota(jnp.int32, (count, count), 0) == lax.broadcasted_iota(
        jnp.int32, (count, count), 1
    )
    return jnp.sum(jnp.where(diagonal, row, 0.0), axis=1, keepdims=True)


def slot_numbers(routes):
    tokens = routes.shape[1]
    onehot = lax.broadcasted_iota(jnp.int32, (128, tokens), 0) == routes
    onehot = jnp.where(onehot, 1.0, 0.0)
    earlier = lax.broadcasted_iota(jnp.int32, (tokens, tokens), 0) < lax.broadcasted_iota(
        jnp.int32, (tokens, tokens), 1
    )
    before = nn_dot(
        onehot.astype(jnp.bfloat16), jnp.where(earlier, 1.0, 0.0).astype(jnp.bfloat16)
    )
    rank = jnp.sum(before * onehot, axis=0, keepdims=True)
    return routes.astype(jnp.float32) * SLOTS + rank


def message_kernel(stream_ref, grad_ref, gain_ref, gate_ref, route_ref, out_ref):
    _, _, expert_in = layer_norm(stream_ref[...], gain_ref[...])
    grad_z = (as_column(gate_ref[...]) * grad_ref[...].astype(jnp.float32)).astype(jnp.bfloat16)
    slots = slot_numbers(route_ref[...]).astype(jnp.int32)
    tables = pack_tables(slots, out_ref.shape[0])
    out_ref[:, :640] = pack_rows(tables, expert_in)
    out_ref[:, 640:] = pack_rows(tables, grad_z)


def ring_places():
    e = lax.axis_index("expert")
    d = lax.axis_index("dp")
    places = dict(
        right=lax.rem(e + 2, 8),
        left=lax.rem(e + 6, 8),
        far=lax.rem(e + 4, 8),
        pair=e + 1 - 2 * lax.rem(e, 2),
    )
    return e, d, d // 8, lax.rem(d, 8), places


def greet_all(d, places):
    barrier = pltpu.get_barrier_semaphore()

    def greet(i, carry):
        pl.semaphore_signal(
            barrier, inc=1, device_id={"dp": lax.rem(d + i, 32)}, device_id_type=MESH
        )
        return carry

    lax.fori_loop(1, 32, greet, 0)
    for name in ("right", "left", "pair"):
        pl.semaphore_signal(
            barrier, inc=1, device_id={"expert": places[name]}, device_id_type=MESH
        )
    pl.semaphore_wait(barrier, 34)


def remote(src, dst, send, recv, **where):
    return pltpu.make_async_remote_copy(
        src_ref=src, dst_ref=dst, send_sem=send, recv_sem=recv, device_id=where, device_id_type=MESH
    )


def dispatch_kernel(
    msg_ref,
    key_ref,
    value_ref,
    query_ref,
    bx_ref,
    bg_ref,
    mid_ref,
    recv,
    stage,
    all_send,
    all_recv,
    own_sem,
    ring_recv,
    ring_send,
    keep_sem,
    rim_send,
    rim_recv,
    rim_keep,
):
    e, d, x, z, places = ring_places()
    width = key_ref.shape[1]
    boxes = (bx_ref, bg_ref)
    greet_all(d, places)

    def message(target):
        return remote(
            msg_ref.at[target],
            recv.at[x, pl.ds(pl.multiple_of(z * 16, 16), 16)],
            all_send.at[target],
            all_recv.at[d],
            dp=target,
        )

    own = pltpu.make_async_copy(
        msg_ref.at[d], recv.at[x, pl.ds(pl.multiple_of(z * 16, 16), 16)], own_sem
    )
    own.start()
    for g in range(4):
        row = lax.rem(x + g, 4) * 8

        def send(i, carry):
            message(row + lax.rem(z + i, 8)).start()
            return carry

        lax.fori_loop(1 if g == 0 else 0, 8, send, 0)

    rim = 48
    tokens = key_ref.shape[0]
    after, before = lax.rem(d + 1, 32), lax.rem(d + 31, 32)
    rims, keeps = [], []
    for i, ref in enumerate((key_ref, value_ref, query_ref)):
        lanes = pl.ds(i * width, width)
        rims.append(
            remote(
                ref.at[pl.ds(tokens - rim, rim)],
                mid_ref.at[pl.ds(0, rim), lanes],
                rim_send.at[i, 0],
                rim_recv.at[i, 0],
                dp=after,
            )
        )
        rims.append(
            remote(
                ref.at[pl.ds(0, rim)],
                mid_ref.at[pl.ds(tokens + rim, rim), lanes],
                rim_send.at[i, 1],
                rim_recv.at[i, 1],
                dp=before,
            )
        )
        keeps.append(
            pltpu.make_async_copy(ref, mid_ref.at[pl.ds(rim, tokens), lanes], rim_keep.at[i])
        )
    for copy in rims + keeps:
        copy.start()

    index = lax.broadcasted_iota(jnp.int32, (8 * SLOTS, 1), 0)
    tables = unpack_tables(index, 128)

    def group(g):
        return lax.rem(x + 4 - g, 4)

    def ring(source, g, kind, where, number, staged=False):
        src = stage.at[g, kind] if staged else boxes[kind].at[source, group(g)]
        return remote(
            src,
            boxes[kind].at[source, group(g)],
            ring_send.at[g, kind, number],
            ring_recv.at[source, group(g), kind],
            expert=places[where],
        )

    sent = []
    for g in range(6):
        if g < 4:
            row = group(g) * 8

            def take(i, carry):
                source = row + lax.rem(z + 8 - i, 8)
                remote(
                    msg_ref.at[source],
                    recv.at[group(g), pl.ds(pl.multiple_of(lax.rem(source, 8) * 16, 16), 16)],
                    all_send.at[source],
                    all_recv.at[source],
                    dp=source,
                ).wait_recv()
                return carry

            lax.fori_loop(1 if g == 0 else 0, 8, take, 0)
            if g == 0:
                own.wait()
            for kind in range(2):
                got = recv[group(g), :, 640 * kind : 640 * (kind + 1)]
                stage[g, kind] = unpack_rows(tables, got).astype(jnp.bfloat16)
                for number, where in enumerate(("right", "left", "pair")):
                    copy = ring(e, g, kind, where, number, True)
                    copy.start()
                    sent.append(copy)
                copy = pltpu.make_async_copy(
                    stage.at[g, kind], boxes[kind].at[e, group(g)], keep_sem.at[g, kind]
                )
                copy.start()
        if 1 <= g < 5:
            h = g - 1
            for name, onward, passed, number in (("left", "right", 0, 3), ("right", "left", 1, 4)):
                source = places[name]
                for kind in range(2):
                    ring(source, h, kind, "right", 0).wait_recv()
                    if kind == passed:
                        copy = ring(source, h, kind, onward, 3)
                        copy.start()
                        sent.append(copy)
                    copy = ring(source, h, kind, "pair", number + 1)
                    copy.start()
                    sent.append(copy)
        if 2 <= g:
            h = g - 2
            for kind in range(2):
                ring(places["far"], h, kind, "right", 0).wait_recv()
                copy = ring(places["far"], h, kind, "pair", 6)
                copy.start()
                sent.append(copy)
    side = lax.rem(e, 2)
    for g in range(4):
        for y in range(4):
            for kind in range(2):
                ring(2 * y + 1 - side, g, kind, "right", 0).wait_recv()
    for copy in sent:
        copy.wait_send()
    for g in range(4):
        for kind in range(2):
            pltpu.make_async_copy(
                stage.at[g, kind], boxes[kind].at[e, group(g)], keep_sem.at[g, kind]
            ).wait()

    def sent_all(i, carry):
        message(lax.rem(d + i, 32)).wait_send()
        return carry

    lax.fori_loop(1, 32, sent_all, 0)
    for copy in rims:
        copy.wait()
    for copy in keeps:
        copy.wait()


def return_kernel(
    back_ref,
    out_ref,
    from_pair,
    mine,
    from_left,
    from_right,
    early,
    packed,
    pair_send,
    pair_recv,
    far_send,
    far_recv,
    near_send,
    near_recv,
    all_send,
    all_recv,
    own_sem,
):
    e, d, x, z, places = ring_places()
    greet_all(d, places)
    right, left, far, pair = (places[name] for name in ("right", "left", "far", "pair"))

    def group(g):
        return lax.rem(x + g, 4)

    order = ((2, far), (1, right), (3, left), (0, e))
    pairs = []
    for step, target in order:
        other = target + pair - e
        copy = remote(
            back_ref.at[other],
            from_pair.at[step],
            pair_send.at[step],
            pair_recv.at[step],
            expert=pair,
        )
        copy.start()
        pairs.append(copy)

    def joined(step, target, g):
        return back_ref[target, group(g)].astype(jnp.float32) + from_pair[step, group(g)].astype(
            jnp.float32
        )

    def far_copy(g):
        return remote(
            mine.at[2, g],
            early.at[g],
            far_send.at[g],
            far_recv.at[g],
            expert=right if g < 2 else left,
        )

    def near_copy(step, g):
        return remote(
            mine.at[step, g],
            (from_left if step == 1 else from_right).at[g],
            near_send.at[step // 2, g],
            near_recv.at[step // 2, g],
            expert=right if step == 1 else left,
        )

    pairs[0].wait_recv()
    for g in (0, 2, 1, 3):
        mine[2, g] = joined(2, far, g).astype(jnp.bfloat16)
        far_copy(g).start()
    pairs[1].wait_recv()
    for g in (2, 3):
        mine[1, g] = joined(1, right, g).astype(jnp.bfloat16)
        near_copy(1, g).start()
    pairs[2].wait_recv()
    for g in (0, 1):
        mine[3, g] = joined(3, left, g).astype(jnp.bfloat16)
        near_copy(3, g).start()
    for g in (0, 1):
        far_copy(g).wait_recv()
        mine[1, g] = (joined(1, right, g) + early[g].astype(jnp.float32)).astype(jnp.bfloat16)
        near_copy(1, g).start()
        far_copy(g + 2).wait_recv()
        mine[3, g + 2] = (joined(3, left, g + 2) + early[g + 2].astype(jnp.float32)).astype(
            jnp.bfloat16
        )
        near_copy(3, g + 2).start()
    pairs[3].wait_recv()
    index = lax.broadcasted_iota(jnp.int32, (1, 8 * SLOTS), 1)
    tables = pack_tables(index, 128)

    def message(g, i):
        place = lax.rem(z + i, 8)
        target = group(g) * 8 + place
        rows = pl.ds(pl.multiple_of(place * 16, 16), 16)
        return remote(
            packed.at[g, rows], out_ref.at[d], all_send.at[target], all_recv.at[d], dp=target
        )

    own = pltpu.make_async_copy(
        packed.at[0, pl.ds(pl.multiple_of(z * 16, 16), 16)], out_ref.at[d], own_sem
    )
    for g in (0, 2, 1, 3):
        near_copy(1, g).wait_recv()
        near_copy(3, g).wait_recv()
        total = (
            joined(0, e, g)
            + from_left[g].astype(jnp.float32)
            + from_right[g].astype(jnp.float32)
        )
        packed[g] = pack_rows(tables, total.astype(jnp.bfloat16))

        def send(i, carry):
            message(g, i).start()
            return carry

        lax.fori_loop(1 if g == 0 else 0, 8, send, 0)
        if g == 0:
            own.start()

    def take(i, carry):
        source = lax.rem(d + i, 32)
        remote(
            packed.at[0, pl.ds(0, 16)],
            out_ref.at[source],
            all_send.at[source],
            all_recv.at[source],
            dp=source,
        ).wait_recv()
        return carry

    lax.fori_loop(1, 32, take, 0)
    own.wait()
    for copy in pairs:
        copy.wait_send()
    for g in range(4):
        far_copy(g).wait_send()
        near_copy(1, g).wait_send()
        near_copy(3, g).wait_send()
        lax.fori_loop(
            1 if g == 0 else 0, 8, lambda i, carry: (message(g, i).wait_send(), carry)[1], 0
        )


def halo_kernel(block_ref, left_ref, mid_ref, right_ref, send_sem, recv_sem, own_sem):
    e = lax.axis_index("expert")
    d = lax.axis_index("dp")
    tokens = block_ref.shape[0]
    rim = (left_ref.shape[0] - tokens) // 2
    places = []
    for down in (-1, 0, 1):
        for over in (-1, 0, 1):
            if down or over:
                places.append((down, over, lax.rem(d + 32 + down, 32), lax.rem(e + 8 + over, 8)))
    barrier = pltpu.get_barrier_semaphore()
    for _, _, row, col in places:
        pl.semaphore_signal(
            barrier, inc=1, device_id={"dp": row, "expert": col}, device_id_type=MESH
        )
    pl.semaphore_wait(barrier, len(places))
    own = pltpu.make_async_copy(block_ref, mid_ref.at[pl.ds(rim, tokens)], own_sem)
    copies = []
    for number, (down, over, row, col) in enumerate(places):
        side = {1: left_ref, 0: mid_ref, -1: right_ref}[over]
        if down == 0:
            src, dst = pl.ds(0, tokens), pl.ds(rim, tokens)
        elif down == 1:
            src, dst = pl.ds(tokens - rim, rim), pl.ds(0, rim)
        else:
            src, dst = pl.ds(0, rim), pl.ds(rim + tokens, rim)
        copies.append(
            remote(
                block_ref.at[src],
                side.at[dst],
                send_sem.at[number],
                recv_sem.at[number],
                dp=row,
                expert=col,
            )
        )
    for number in (3, 4, 0, 2, 5, 7, 1, 6):
        copies[number].start()
    own.start()
    for copy in copies:
        copy.wait()
    own.wait()


def head_lanes(head, size, width):
    start = head * size
    low = start // 128 * 128
    high = min((start + size + 127) // 128 * 128, width)
    return start, low, high


def lane_mask(head, size, low, high):
    lanes = lax.broadcasted_iota(jnp.int32, (1, high - low), 1) + low
    return (lanes >= head * size) & (lanes < (head + 1) * size)


def nt_dot(left, right):
    return lax.dot_general(left, right, (((1,), (1,)), ((), ())), preferred_element_type=jnp.float32)


def nn_dot(left, right):
    return jnp.dot(left, right, preferred_element_type=jnp.float32)


def window_bias(band, cols, rows_total, cols_total):
    row_index = lax.axis_index("dp")
    col_index = lax.axis_index("expert")
    side = (band + 2 * RAD) * cols
    shape = (band * cols, 3 * side)
    shift = cols.bit_length() - 1
    own = lax.broadcasted_iota(jnp.int32, shape, 0)
    far = lax.broadcasted_iota(jnp.int32, shape, 1)
    part = (far >= side).astype(jnp.int32) + (far >= 2 * side).astype(jnp.int32)
    within = far - side * part
    far_row = (within >> shift) - RAD
    far_col = (within & (cols - 1)) + cols * (part - 1)
    own_row = own >> shift
    own_col = own & (cols - 1)
    abs_row = far_row + row_index * band
    abs_col = far_col + col_index * cols
    fine = (
        (jnp.abs(far_row - own_row) <= RAD)
        & (jnp.abs(far_col - own_col) <= RAD)
        & (abs_row >= 0)
        & (abs_row < rows_total)
        & (abs_col >= 0)
        & (abs_col < cols_total)
    )
    return jnp.where(fine, 0.0, NEG_LARGE)


def tall(refs, low, high):
    return jnp.concatenate([ref[:, low:high] for ref in refs], axis=0)


def forward_kernel(sizes, query_ref, left_ref, mid_ref, right_ref, att_ref, stats_ref, bias_ref):
    band, cols, rows_total, cols_total = sizes
    width = query_ref.shape[1]
    size = width // HEADS
    scale = size ** (-0.5)
    refs = (left_ref, mid_ref, right_ref)
    bias_ref[...] = window_bias(band, cols, rows_total, cols_total)
    att_ref[...] = jnp.zeros_like(att_ref)
    lanes = lax.broadcasted_iota(jnp.int32, stats_ref.shape, 1)
    stats = jnp.zeros(stats_ref.shape, jnp.float32)
    for head in range(HEADS):
        start, low, high = head_lanes(head, size, width)
        mask = lane_mask(head, size, low, high)
        queries = query_ref[:, low:high] * mask.astype(jnp.bfloat16)
        scores = nt_dot(queries, tall(refs, low, high)) * scale + bias_ref[...]
        peak = jnp.max(scores, axis=-1, keepdims=True)
        log_total = peak + jnp.log(jnp.sum(jnp.exp(scores - peak), axis=-1, keepdims=True))
        probs_low = jnp.exp(scores - log_total).astype(jnp.bfloat16)
        attended = nn_dot(probs_low, tall(refs, width + low, width + high))
        att_ref[:, low:high] += jnp.where(mask, attended, 0.0)
        stats = jnp.where(lanes == head, log_total, stats)
    stats_ref[...] = stats


def split_three(values):
    first = values.astype(jnp.bfloat16)
    rest = values - first.astype(jnp.float32)
    second = rest.astype(jnp.bfloat16)
    third = (rest - second.astype(jnp.float32)).astype(jnp.bfloat16)
    return first, second, third


def stream_kernel(
    stream_ref, grad_ref, gain_ref, route_ref, back_ref, att_ref, stats_ref, plain_ref, packed_ref
):
    width = stream_ref.shape[1]
    size = width // HEADS
    gain = gain_ref[...]
    normed, inv_std, _ = layer_norm(stream_ref[...], gain)
    slots = as_column(slot_numbers(route_ref[...])).astype(jnp.int32)
    grad_in = unpack_rows(unpack_tables(slots, back_ref.shape[0]), back_ref[...])
    grad_stream = (
        grad_ref[...].astype(jnp.float32) + norm_backward(grad_in, normed, inv_std, gain)
    ).astype(jnp.bfloat16)
    plain_ref[...] = grad_stream
    packed_ref[:, :width] = grad_stream
    products = grad_stream.astype(jnp.float32) * att_ref[...]
    feature = lax.broadcasted_iota(jnp.int32, (width, 128), 0)
    first = lax.broadcasted_iota(jnp.int32, (width, 128), 1) * size
    owner = jnp.where((feature >= first) & (feature < first + size), 1.0, 0.0).astype(jnp.bfloat16)
    delta = sum(nn_dot(piece, owner) for piece in split_three(products))
    source = lax.broadcasted_iota(jnp.int32, (128, 128), 0)
    target = lax.broadcasted_iota(jnp.int32, (128, 128), 1)
    total = jnp.zeros(delta.shape, jnp.float32)
    pieces = split_three(stats_ref[...]) + split_three(delta)
    for place, piece in enumerate(pieces):
        move = (target == source + place * HEADS) & (source < HEADS)
        total = total + nn_dot(piece, jnp.where(move, 1.0, 0.0).astype(jnp.bfloat16))
    packed_ref[:, width:] = total.astype(jnp.bfloat16)


def backward_kernel(
    sizes,
    left_ref,
    mid_ref,
    right_ref,
    gleft_ref,
    gmid_ref,
    gright_ref,
    gq_ref,
    gk_ref,
    gv_ref,
    bias_ref,
    acc_q,
    acc_k,
    acc_v,
):
    band, cols, rows_total, cols_total = sizes
    width = gq_ref.shape[1]
    size = width // HEADS
    scale = size ** (-0.5)
    tokens = band * cols
    own = slice(RAD * cols, RAD * cols + tokens)
    refs = (left_ref, mid_ref, right_ref)
    grefs = (gleft_ref, gmid_ref, gright_ref)
    bias_ref[...] = window_bias(band, cols, rows_total, cols_total)
    for acc in (acc_q, acc_k, acc_v):
        acc[...] = jnp.zeros_like(acc)
    row = lax.broadcasted_iota(jnp.int32, (2 * HEADS, 128), 0)
    lane = lax.broadcasted_iota(jnp.int32, (2 * HEADS, 128), 1)
    base = jnp.where(row < HEADS, row, row + 2 * HEADS)
    pick = jnp.where(
        (lane == base) | (lane == base + HEADS) | (lane == base + 2 * HEADS), 1.0, 0.0
    ).astype(jnp.bfloat16)
    stats_far = nt_dot(pick, tall(grefs, width, width + 128))
    stats_own = nt_dot(gmid_ref[own, width : width + 128], pick)
    for head in range(HEADS):
        start, low, high = head_lanes(head, size, width)
        mask = lane_mask(head, size, low, high)
        mask_low = mask.astype(jnp.bfloat16)
        keys = tall(refs, low, high)
        values = tall(refs, width + low, width + high)
        queries = tall(refs, 2 * width + low, 2 * width + high)
        grads = tall(grefs, low, high)
        bias = bias_ref[...]
        own_key = mid_ref[own, low:high] * mask_low
        own_value = mid_ref[own, width + low : width + high] * mask_low
        own_query = mid_ref[own, 2 * width + low : 2 * width + high] * mask_low
        own_grad = gmid_ref[own, low:high] * mask_low

        probs = jnp.exp(
            nt_dot(own_query, keys) * scale + bias - stats_own[:, head : head + 1]
        )
        grad_probs = nt_dot(own_grad, values)
        grad_scores = (
            probs * (grad_probs - stats_own[:, HEADS + head : HEADS + head + 1])
        ).astype(jnp.bfloat16)
        acc_q[:, low:high] += jnp.where(mask, nn_dot(grad_scores, keys), 0.0)

        probs = jnp.exp(
            nt_dot(own_key, queries) * scale + bias - stats_far[head : head + 1, :]
        )
        acc_v[:, low:high] += jnp.where(mask, nn_dot(probs.astype(jnp.bfloat16), grads), 0.0)
        grad_probs = nt_dot(own_value, grads)
        grad_scores = (
            probs * (grad_probs - stats_far[HEADS + head : HEADS + head + 1, :])
        ).astype(jnp.bfloat16)
        acc_k[:, low:high] += jnp.where(mask, nn_dot(grad_scores, queries), 0.0)
    gq_ref[...] = (acc_q[...] * scale).astype(jnp.bfloat16)
    gk_ref[...] = (acc_k[...] * scale).astype(jnp.bfloat16)
    gv_ref[...] = acc_v[...].astype(jnp.bfloat16)


def vmem():
    return pl.BlockSpec(memory_space=pltpu.VMEM)


def sides(mid):
    count = lax.axis_size("expert")
    forward = [(i, i + 1) for i in range(count - 1)]
    backward = [(b, a) for a, b in forward]
    return lax.ppermute(mid, "expert", forward), mid, lax.ppermute(mid, "expert", backward)


def anywhere():
    return pl.BlockSpec(memory_space=pl.ANY)


def params(collective_id=None):
    if collective_id is None:
        return pltpu.CompilerParams(vmem_limit_bytes=VMEM_LIMIT)
    return pltpu.CompilerParams(
        vmem_limit_bytes=VMEM_LIMIT, collective_id=collective_id, has_side_effects=True
    )


def shaped(shape, kind=jnp.bfloat16):
    return jax.ShapeDtypeStruct(shape, kind)


def body(
    query_act,
    key_act,
    value_act,
    stream,
    grad_out,
    norm_gain,
    route_ids,
    gate_prob,
    weight_in,
    weight_out,
):
    band, cols, width = stream.shape
    tokens = band * cols
    experts = lax.axis_size("dp")
    col_parts = lax.axis_size("expert")
    sizes = (band, cols, band * experts, cols * col_parts)
    side = (band + 2 * RAD) * cols
    dma = pltpu.SemaphoreType.DMA
    flat_query, flat_key, flat_value, flat_stream, flat_grad = (
        array.reshape(tokens, width) for array in (query_act, key_act, value_act, stream, grad_out)
    )
    gain = norm_gain.reshape(1, width)
    routes = route_ids.reshape(1, tokens)
    messages = pl.pallas_call(
        message_kernel,
        out_shape=shaped((experts * 16, 1280)),
        in_specs=[vmem()] * 5,
        out_specs=vmem(),
        compiler_params=params(),
        name="messages",
    )(flat_stream, flat_grad, gain, gate_prob.reshape(1, tokens), routes)
    rows_in, rows_grad, mid = pl.pallas_call(
        dispatch_kernel,
        out_shape=(
            shaped((8, 4, 48, width)),
            shaped((8, 4, 48, width)),
            shaped((side, 3 * width)),
        ),
        in_specs=[vmem()] + [anywhere()] * 3,
        out_specs=(anywhere(),) * 3,
        scratch_shapes=[
            pltpu.VMEM((4, 128, 1280), jnp.bfloat16),
            pltpu.VMEM((4, 2, 48, width), jnp.bfloat16),
            dma((32,)),
            dma((32,)),
            dma,
            dma((8, 4, 2)),
            dma((4, 2, 7)),
            dma((4, 2)),
            dma((3, 2)),
            dma((3, 2)),
            dma((3,)),
        ],
        compiler_params=params(1),
        name="dispatch",
    )(messages.reshape(experts, 16, 1280), flat_key, flat_value, flat_query)
    near = sides(mid)
    grad_first, grad_second, back_terms = expert_grads(
        rows_in.reshape(-1, width), rows_grad.reshape(-1, width), weight_in[0], weight_out[0]
    )
    attended, log_total = pl.pallas_call(
        functools.partial(forward_kernel, sizes),
        out_shape=(shaped((tokens, width), jnp.float32), shaped((tokens, 128), jnp.float32)),
        in_specs=[vmem()] * 4,
        out_specs=(vmem(), vmem()),
        scratch_shapes=[pltpu.VMEM((tokens, 3 * side), jnp.float32)],
        compiler_params=params(),
        name="attend",
    )(flat_query, *near)
    returned = pl.pallas_call(
        return_kernel,
        out_shape=shaped((experts, 16, 640)),
        in_specs=[vmem()],
        out_specs=vmem(),
        scratch_shapes=[pltpu.VMEM((4, 4, 48, width), jnp.bfloat16)] * 2
        + [pltpu.VMEM((4, 48, width), jnp.bfloat16)] * 3
        + [
            pltpu.VMEM((4, 128, 640), jnp.bfloat16),
            dma((4,)),
            dma((4,)),
            dma((4,)),
            dma((4,)),
            dma((2, 4)),
            dma((2, 4)),
            dma((32,)),
            dma((32,)),
            dma,
        ],
        compiler_params=params(2),
        name="give_back",
    )(back_terms.astype(jnp.bfloat16).reshape(8, 4, 48, width))
    plain, packed = pl.pallas_call(
        stream_kernel,
        out_shape=(shaped((tokens, width)), shaped((tokens, width + 128))),
        in_specs=[vmem()] * 7,
        out_specs=(vmem(), vmem()),
        compiler_params=params(),
        name="stream_grad",
    )(flat_stream, flat_grad, gain, routes, returned.reshape(-1, 640), attended, log_total)
    far = pl.pallas_call(
        halo_kernel,
        out_shape=(shaped((side, width + 128)),) * 3,
        in_specs=[vmem()],
        out_specs=(vmem(),) * 3,
        scratch_shapes=[dma((8,)), dma((8,)), dma],
        compiler_params=params(3),
        name="halo",
    )(packed)
    grad_query, grad_key, grad_value = pl.pallas_call(
        functools.partial(backward_kernel, sizes),
        out_shape=(shaped((tokens, width)),) * 3,
        in_specs=[vmem()] * 6,
        out_specs=(vmem(),) * 3,
        scratch_shapes=[pltpu.VMEM((tokens, 3 * side), jnp.float32)]
        + [pltpu.VMEM((tokens, width), jnp.float32)] * 3,
        compiler_params=params(),
        name="attend_back",
    )(*near, *far)
    shape = (band, cols, width)
    return (
        grad_query.reshape(shape),
        grad_key.reshape(shape),
        grad_value.reshape(shape),
        plain.reshape(shape),
        grad_first[None],
        grad_second[None],
    )


def solution(mesh):
    in_specs = (
        P("dp", "expert", None),
        P("dp", "expert", None),
        P("dp", "expert", None),
        P("dp", "expert", None),
        P("dp", "expert", None),
        P(),
        P("dp", "expert", None, None),
        P("dp", "expert", None),
        P("dp", None, "expert"),
        P("dp", "expert", None),
    )
    out_specs = (
        P("dp", "expert", None),
        P("dp", "expert", None),
        P("dp", "expert", None),
        P("dp", "expert", None),
        P("dp", None, "expert"),
        P("dp", "expert", None),
    )
    return jax.shard_map(body, mesh=mesh, in_specs=in_specs, out_specs=out_specs, check_vma=False)
```

```python
import functools

import jax
import jax.numpy as jnp
from jax import lax
from jax.experimental import pallas as pl
from jax.experimental.pallas import tpu as pltpu
from jax.sharding import PartitionSpec as P

HEADS = 16
RAD = 6
SLOTS = 6
MESH = pl.DeviceIdType.MESH
VMEM_LIMIT = 60 * 1024 * 1024


LN_EPS = 1e-05
ROOT_HALF = 0.7071067811865476
INV_ROOT_TAU = 0.3989422804014327
NEG_LARGE = -1e30


def gelu_value(values):
    return 0.5 * values * (1.0 + lax.erf(values * ROOT_HALF))


def gelu_slope(values):
    return (
        0.5 * (1.0 + lax.erf(values * ROOT_HALF))
        + values * jnp.exp(-0.5 * values * values) * INV_ROOT_TAU
    )


def layer_norm(stream, norm_gain):
    values = stream.astype(jnp.float32)
    center = values - jnp.mean(values, axis=-1, keepdims=True)
    inv_std = lax.rsqrt(jnp.mean(center * center, axis=-1, keepdims=True) + LN_EPS)
    normed = center * inv_std
    return (normed, inv_std, (normed * norm_gain).astype(jnp.bfloat16))


def norm_backward(grad_in, normed, inv_std, norm_gain):
    scaled = grad_in * norm_gain
    centered = scaled - jnp.mean(scaled, axis=-1, keepdims=True)
    return inv_std * (centered - normed * jnp.mean(scaled * normed, axis=-1, keepdims=True))


def unit_places(index, first):
    place = index % 16
    block = index // 16
    rank = place - first
    return jnp.where((rank >= 0) & (rank < SLOTS), block * SLOTS + rank, -1)


def slot_rows(index):
    place = index % 16
    block = index // 16
    tail = jnp.where(place >= 12, block * SLOTS + place - 12, -1)
    late = jnp.where((place == 12) | (place == 13), block * SLOTS + place - 8, -1)
    last = jnp.where(place >= 14, block * SLOTS + place - 10, -1)
    return (unit_places(index, 0), unit_places(index, 6), tail, late, last)


def pack_tables(slots, rows):
    index = lax.broadcasted_iota(jnp.int32, (rows, 1), 0)
    return [jnp.where(held == slots, 1.0, 0.0).astype(jnp.bfloat16) for held in slot_rows(index)]


def unpack_tables(slots, rows):
    index = lax.broadcasted_iota(jnp.int32, (1, rows), 1)
    return [jnp.where(held == slots, 1.0, 0.0).astype(jnp.bfloat16) for held in slot_rows(index)]


def pack_rows(tables, values):
    t0, t1, t2, t3, t4 = tables
    chunk = [values[:, 128 * i : 128 * (i + 1)] for i in range(10, 13)]
    tail = jnp.concatenate(
        [
            nn_dot(t2, values[:, 1280:1664]),
            nn_dot(t3, chunk[0]) + nn_dot(t4, chunk[1]),
            nn_dot(t3, chunk[2]),
        ],
        axis=1,
    )
    return (nn_dot(t0, values[:, :640]) + nn_dot(t1, values[:, 640:1280]) + tail).astype(
        jnp.bfloat16
    )


def unpack_rows(tables, packed):
    t0, t1, t2, t3, t4 = tables
    third, fourth = packed[:, 384:512], packed[:, 512:640]
    extra = jnp.concatenate([nn_dot(t3, third), nn_dot(t4, third), nn_dot(t3, fourth)], axis=1)
    return jnp.concatenate(
        [nn_dot(t0, packed), nn_dot(t1, packed), nn_dot(t2, packed[:, :384]) + extra], axis=1
    )


def as_column(row):
    count = row.shape[1]
    diagonal = lax.broadcasted_iota(jnp.int32, (count, count), 0) == lax.broadcasted_iota(
        jnp.int32, (count, count), 1
    )
    return jnp.sum(jnp.where(diagonal, row, 0.0), axis=1, keepdims=True)


def slot_numbers(routes):
    tokens = routes.shape[1]
    onehot = lax.broadcasted_iota(jnp.int32, (128, tokens), 0) == routes
    onehot = jnp.where(onehot, 1.0, 0.0)
    earlier = lax.broadcasted_iota(jnp.int32, (tokens, tokens), 0) < lax.broadcasted_iota(
        jnp.int32, (tokens, tokens), 1
    )
    before = nn_dot(
        onehot.astype(jnp.bfloat16), jnp.where(earlier, 1.0, 0.0).astype(jnp.bfloat16)
    )
    rank = jnp.sum(before * onehot, axis=0, keepdims=True)
    return routes.astype(jnp.float32) * SLOTS + rank


def write_messages(stream, grad, gain, gate, route, out_ref):
    _, _, expert_in = layer_norm(stream, gain)
    grad_z = (as_column(gate) * grad.astype(jnp.float32)).astype(jnp.bfloat16)
    slots = slot_numbers(route).astype(jnp.int32)
    tables = pack_tables(slots, out_ref.shape[0])
    out_ref[:, :640] = pack_rows(tables, expert_in)
    out_ref[:, 640:] = pack_rows(tables, grad_z)


def ring_places():
    e = lax.axis_index("expert")
    d = lax.axis_index("dp")
    places = dict(
        right=lax.rem(e + 2, 8),
        left=lax.rem(e + 6, 8),
        far=lax.rem(e + 4, 8),
        pair=e + 1 - 2 * lax.rem(e, 2),
        beside=lax.rem(e + 7 + 2 * lax.rem(e, 2), 8),
    )
    return e, d, d // 8, lax.rem(d, 8), places


def around(e, d):
    places = []
    for down, over in ((0, 1), (0, -1), (-1, 0), (1, 0), (-1, -1), (-1, 1), (1, -1), (1, 1)):
        places.append((down, over, lax.rem(d + 32 + down, 32), lax.rem(e + 8 + over, 8)))
    return places


def greet_all(e, d, places):
    barrier = pltpu.get_barrier_semaphore()

    def greet(i, carry):
        pl.semaphore_signal(
            barrier, inc=1, device_id={"dp": lax.rem(d + i, 32)}, device_id_type=MESH
        )
        return carry

    lax.fori_loop(1, 32, greet, 0)
    for name in ("right", "left", "pair", "beside"):
        pl.semaphore_signal(
            barrier, inc=1, device_id={"expert": places[name]}, device_id_type=MESH
        )
    for down, over, row, col in around(e, d):
        if down and over:
            pl.semaphore_signal(
                barrier, inc=1, device_id={"dp": row, "expert": col}, device_id_type=MESH
            )
    pl.semaphore_wait(barrier, 39)


def remote(src, dst, send, recv, **where):
    return pltpu.make_async_remote_copy(
        src_ref=src, dst_ref=dst, send_sem=send, recv_sem=recv, device_id=where, device_id_type=MESH
    )


def tn_dot(left, right):
    return lax.dot_general(left, right, (((0,), (0,)), ((), ())), preferred_element_type=jnp.float32)


def rim_slices(down, tokens, rim):
    if down == 0:
        return pl.ds(0, tokens), pl.ds(rim, tokens)
    if down == 1:
        return pl.ds(tokens - rim, rim), pl.ds(0, rim)
    return pl.ds(0, rim), pl.ds(rim + tokens, rim)


def expert_kernel(
    sizes,
    stream_hbm,
    grad_hbm,
    gain_ref,
    gate_ref,
    route_ref,
    key_hbm,
    value_hbm,
    query_hbm,
    first_hbm,
    second_hbm,
    left_hbm,
    mid_hbm,
    right_hbm,
    out_ref,
    att_ref,
    stats_ref,
    grad_first_hbm,
    grad_second_hbm,
    stream_v,
    grad_v,
    first_v,
    second_v,
    msg,
    recv,
    bx,
    bg,
    hidden,
    grad_pre,
    back,
    from_pair,
    mine,
    from_left,
    from_right,
    early,
    packed,
    left_v,
    mid_v,
    right_v,
    bias_ref,
    grad_first_v,
    grad_second_v,
    load_sem,
    store_sem,
    halo_send,
    halo_recv,
    halo_keep,
    halo_out,
    all_send,
    all_recv,
    own_sem,
    ring_send,
    ring_recv,
    pair_send,
    pair_recv,
    far_send,
    far_recv,
    near_send,
    near_recv,
    home_send,
    home_recv,
    home_sem,
):
    e, d, x, z, places = ring_places()
    right, left, far, pair = (places[name] for name in ("right", "left", "far", "pair"))
    tokens, width = stream_hbm.shape
    rim = RAD * sizes[1]
    boxes = (bx, bg)
    sent = []

    loads = [
        pltpu.make_async_copy(source, target, load_sem.at[i])
        for i, (source, target) in enumerate(
            (
                (stream_hbm, stream_v),
                (grad_hbm, grad_v),
                (first_hbm, first_v),
                (second_hbm, second_v),
            )
        )
    ]
    lanes = [pl.ds(i * width, width) for i in range(3)]
    sources = (key_hbm, value_hbm, query_hbm)
    keeps = [
        pltpu.make_async_copy(
            sources[i], mid_v.at[pl.ds(rim, tokens), lanes[i]], halo_keep.at[i]
        )
        for i in range(3)
    ]
    for copy in loads + keeps:
        copy.start()
    greet_all(e, d, places)

    halos = []
    for number, (down, over, row, col) in enumerate(around(e, d)):
        side = {1: left_v, 0: mid_v, -1: right_v}[over]
        src, dst = rim_slices(down, tokens, rim)
        for i in range(3):
            halos.append(
                remote(
                    sources[i].at[src],
                    side.at[dst, lanes[i]],
                    halo_send.at[i, number],
                    halo_recv.at[i, number],
                    dp=row,
                    expert=col,
                )
            )
    for copy in halos[:6]:
        copy.start()

    loads[0].wait()
    loads[1].wait()
    write_messages(stream_v[...], grad_v[...], gain_ref[...], gate_ref[...], route_ref[...], msg)

    def rows16(index):
        return pl.ds(pl.multiple_of(index * 16, 16), 16)

    def rows48(index):
        return pl.ds(pl.multiple_of(index * 48, 16), 48)

    def message(target):
        return remote(
            msg.at[rows16(target)],
            recv.at[x, rows16(z)],
            all_send.at[target],
            all_recv.at[d],
            dp=target,
        )

    own = pltpu.make_async_copy(msg.at[rows16(d)], recv.at[x, rows16(z)], own_sem)
    own.start()
    for g in range(4):
        row = lax.rem(x + g, 4) * 8

        def send(i, carry):
            message(row + lax.rem(z + i, 8)).start()
            return carry

        lax.fori_loop(1 if g == 0 else 0, 8, send, 0)
    for copy in halos[6:]:
        copy.start()

    index = lax.broadcasted_iota(jnp.int32, (8 * SLOTS, 1), 0)
    unpacking = unpack_tables(index, 128)
    index = lax.broadcasted_iota(jnp.int32, (1, 8 * SLOTS), 1)
    packing = pack_tables(index, 128)

    def group(g):
        return lax.rem(x + 4 - g, 4)

    def ring(source, g, kind, where, number):
        block = boxes[kind].at[group(g), rows48(source)]
        return remote(
            block,
            block,
            ring_send.at[g, kind, number],
            ring_recv.at[source, g, kind],
            expert=places[where],
        )

    def go(copy):
        copy.start()
        sent.append(copy)

    def arrive(g):
        row = group(g) * 8

        def take(i, carry):
            source = row + lax.rem(z + 8 - i, 8)
            remote(
                msg.at[rows16(source)],
                recv.at[group(g), rows16(lax.rem(source, 8))],
                all_send.at[source],
                all_recv.at[source],
                dp=source,
            ).wait_recv()
            return carry

        lax.fori_loop(1 if g == 0 else 0, 8, take, 0)
        if g == 0:
            own.wait()
        for kind in range(2):
            got = recv[group(g), :, 640 * kind : 640 * (kind + 1)]
            boxes[kind][group(g), rows48(e), :] = unpack_rows(unpacking, got).astype(jnp.bfloat16)
            for number, where in enumerate(("right", "left", "pair")):
                go(ring(e, g, kind, where, number))

    def relay(g):
        for name, onward, passed, number in (("left", "right", 0, 4), ("right", "left", 1, 5)):
            for kind in range(2):
                ring(places[name], g, kind, "right", 0).wait_recv()
                if kind == passed:
                    go(ring(places[name], g, kind, onward, 3))
                go(ring(places[name], g, kind, "pair", number))

    def finish(g):
        for kind in range(2):
            ring(far, g, kind, "right", 0).wait_recv()
            go(ring(far, g, kind, "pair", 6))

    side_of = lax.rem(e, 2)
    steps = ((2, far), (1, right), (3, left), (0, e))

    def pair_copy(step, target, g):
        return remote(
            back.at[group(g), rows48(target + pair - e)],
            from_pair.at[step, g],
            pair_send.at[step, g],
            pair_recv.at[step, g],
            expert=pair,
        )

    def work(g):
        for y in range(4):
            for kind in range(2):
                ring(2 * y + 1 - side_of, g, kind, "right", 0).wait_recv()
        at = group(g)
        for low in range(0, 512, 256):
            cut = slice(low, low + 256)
            pre_act = nn_dot(bx[at], first_v[:, cut])
            grad_hidden = nt_dot(bg[at], second_v[cut, :])
            hidden[at, :, cut] = gelu_value(pre_act).astype(jnp.bfloat16)
            grad_pre[at, :, cut] = (grad_hidden * gelu_slope(pre_act)).astype(jnp.bfloat16)
        for low in range(0, width, 512):
            cut = slice(low, min(low + 512, width))
            back[at, :, cut] = nt_dot(grad_pre[at], first_v[cut, :]).astype(jnp.bfloat16)
        for step, target in steps:
            go(pair_copy(step, target, g))

    def joined(step, target, g):
        return back[group(g), rows48(target), :].astype(jnp.float32) + from_pair[step, g].astype(
            jnp.float32
        )

    def far_copy(g):
        return remote(
            mine.at[2, g],
            early.at[g],
            far_send.at[g],
            far_recv.at[g],
            expert=left if g % 2 else right,
        )

    def near_copy(step, g):
        return remote(
            mine.at[step, g],
            (from_left if step == 1 else from_right).at[g],
            near_send.at[step // 2, g],
            near_recv.at[step // 2, g],
            expert=right if step == 1 else left,
        )

    def share(g):
        for step, target in steps:
            pair_copy(step, target, g).wait_recv()
        mine[2, g] = joined(2, far, g).astype(jnp.bfloat16)
        go(far_copy(g))
        step, target = (1, right) if g % 2 else (3, left)
        mine[step, g] = joined(step, target, g).astype(jnp.bfloat16)
        go(near_copy(step, g))

    def add_far(g):
        far_copy(g).wait_recv()
        step, target = (3, left) if g % 2 else (1, right)
        mine[step, g] = (joined(step, target, g) + early[g].astype(jnp.float32)).astype(
            jnp.bfloat16
        )
        go(near_copy(step, g))

    def home(g, i):
        place = lax.rem(z + i, 8)
        target = group(g) * 8 + place
        return remote(
            packed.at[g, rows16(place)],
            out_ref.at[d],
            home_send.at[target],
            home_recv.at[d],
            dp=target,
        )

    home_own = pltpu.make_async_copy(packed.at[0, rows16(z)], out_ref.at[d], home_sem)

    def give(g):
        near_copy(1, g).wait_recv()
        near_copy(3, g).wait_recv()
        total = (
            joined(0, e, g) + from_left[g].astype(jnp.float32) + from_right[g].astype(jnp.float32)
        )
        packed[g] = pack_rows(packing, total.astype(jnp.bfloat16))

        def send(i, carry):
            home(g, i).start()
            return carry

        lax.fori_loop(1 if g == 0 else 0, 8, send, 0)
        if g == 0:
            home_own.start()

    outs = [
        pltpu.make_async_copy(source, target, halo_out.at[i])
        for i, (source, target) in enumerate(
            ((left_v, left_hbm), (mid_v, mid_hbm), (right_v, right_hbm))
        )
    ]

    def look():
        for copy in keeps:
            copy.wait()
        for copy in halos:
            copy.wait_recv()
        for copy in outs:
            copy.start()
        bias_ref[...] = window_bias(*sizes)
        att_ref[...] = jnp.zeros_like(att_ref)
        stats_ref[...] = jnp.zeros_like(stats_ref)

    def attend(heads):
        own_rows = slice(rim, rim + tokens)
        refs = (left_v, mid_v, right_v)
        size = width // HEADS
        scale = size ** (-0.5)
        lane = lax.broadcasted_iota(jnp.int32, stats_ref.shape, 1)
        stats = stats_ref[...]
        for head in heads:
            start, low, high = head_lanes(head, size, width)
            mask = lane_mask(head, size, low, high)
            queries = mid_v[own_rows, 2 * width + low : 2 * width + high] * mask.astype(
                jnp.bfloat16
            )
            scores = nt_dot(queries, tall(refs, low, high)) * scale + bias_ref[...]
            peak = jnp.max(scores, axis=-1, keepdims=True)
            log_total = peak + jnp.log(jnp.sum(jnp.exp(scores - peak), axis=-1, keepdims=True))
            probs_low = jnp.exp(scores - log_total).astype(jnp.bfloat16)
            attended = nn_dot(probs_low, tall(refs, width + low, width + high))
            att_ref[:, low:high] += jnp.where(mask, attended, 0.0)
            stats = jnp.where(lane == head, log_total, stats)
        stats_ref[...] = stats

    def first_grad(lows):
        for low in lows:
            cut = slice(low, min(low + 256, width))
            grad_first_v[cut, :] = sum(
                tn_dot(bx[g, :, cut], grad_pre[g]) for g in range(4)
            ).astype(jnp.bfloat16)

    def second_grad(low):
        cut = slice(low, low + 256)
        grad_second_v[cut, :] = sum(
            tn_dot(hidden[g, :, cut], bg[g]) for g in range(4)
        ).astype(jnp.bfloat16)

    stores = [
        pltpu.make_async_copy(grad_first_v, grad_first_hbm, store_sem.at[0]),
        pltpu.make_async_copy(grad_second_v, grad_second_hbm, store_sem.at[1]),
    ]

    arrive(0)
    arrive(1)
    relay(0)
    arrive(2)
    finish(0)
    relay(1)
    loads[2].wait()
    loads[3].wait()
    work(0)
    arrive(3)
    look()
    attend(range(0, 4))
    finish(1)
    relay(2)
    share(0)
    work(1)
    attend(range(4, 8))
    finish(2)
    relay(3)
    add_far(0)
    share(1)
    work(2)
    attend(range(8, 12))
    finish(3)
    give(0)
    add_far(1)
    share(2)
    work(3)
    share(3)
    give(1)
    add_far(2)
    attend(range(12, 16))
    add_far(3)
    give(2)
    first_grad(range(0, 1024, 256))
    give(3)
    first_grad(range(1024, width, 256))
    stores[0].start()
    second_grad(0)
    second_grad(256)
    stores[1].start()

    def take_home(i, carry):
        source = lax.rem(d + i, 32)
        remote(
            packed.at[0, pl.ds(0, 16)],
            out_ref.at[source],
            home_send.at[source],
            home_recv.at[source],
            dp=source,
        ).wait_recv()
        return carry

    lax.fori_loop(1, 32, take_home, 0)
    home_own.wait()
    for copy in sent + halos:
        copy.wait_send()

    def sent_all(i, carry):
        message(lax.rem(d + i, 32)).wait_send()
        return carry

    lax.fori_loop(1, 32, sent_all, 0)
    for g in range(4):

        def sent_home(i, carry):
            home(g, i).wait_send()
            return carry

        lax.fori_loop(1 if g == 0 else 0, 8, sent_home, 0)
    for copy in outs + stores:
        copy.wait()


def halo_kernel(block_ref, left_ref, mid_ref, right_ref, send_sem, recv_sem, own_sem):
    e = lax.axis_index("expert")
    d = lax.axis_index("dp")
    tokens = block_ref.shape[0]
    rim = (left_ref.shape[0] - tokens) // 2
    places = around(e, d)
    barrier = pltpu.get_barrier_semaphore()
    for _, _, row, col in places:
        pl.semaphore_signal(
            barrier, inc=1, device_id={"dp": row, "expert": col}, device_id_type=MESH
        )
    pl.semaphore_wait(barrier, len(places))
    own = pltpu.make_async_copy(block_ref, mid_ref.at[pl.ds(rim, tokens)], own_sem)
    copies = []
    for number, (down, over, row, col) in enumerate(places):
        side = {1: left_ref, 0: mid_ref, -1: right_ref}[over]
        src, dst = rim_slices(down, tokens, rim)
        copies.append(
            remote(
                block_ref.at[src],
                side.at[dst],
                send_sem.at[number],
                recv_sem.at[number],
                dp=row,
                expert=col,
            )
        )
    for copy in copies:
        copy.start()
    own.start()
    for copy in copies:
        copy.wait()
    own.wait()


def head_lanes(head, size, width):
    start = head * size
    low = start // 128 * 128
    high = min((start + size + 127) // 128 * 128, width)
    return start, low, high


def lane_mask(head, size, low, high):
    lanes = lax.broadcasted_iota(jnp.int32, (1, high - low), 1) + low
    return (lanes >= head * size) & (lanes < (head + 1) * size)


def nt_dot(left, right):
    return lax.dot_general(left, right, (((1,), (1,)), ((), ())), preferred_element_type=jnp.float32)


def nn_dot(left, right):
    return jnp.dot(left, right, preferred_element_type=jnp.float32)


def window_bias(band, cols, rows_total, cols_total):
    row_index = lax.axis_index("dp")
    col_index = lax.axis_index("expert")
    side = (band + 2 * RAD) * cols
    shape = (band * cols, 3 * side)
    shift = cols.bit_length() - 1
    own = lax.broadcasted_iota(jnp.int32, shape, 0)
    far = lax.broadcasted_iota(jnp.int32, shape, 1)
    part = (far >= side).astype(jnp.int32) + (far >= 2 * side).astype(jnp.int32)
    within = far - side * part
    far_row = (within >> shift) - RAD
    far_col = (within & (cols - 1)) + cols * (part - 1)
    own_row = own >> shift
    own_col = own & (cols - 1)
    abs_row = far_row + row_index * band
    abs_col = far_col + col_index * cols
    fine = (
        (jnp.abs(far_row - own_row) <= RAD)
        & (jnp.abs(far_col - own_col) <= RAD)
        & (abs_row >= 0)
        & (abs_row < rows_total)
        & (abs_col >= 0)
        & (abs_col < cols_total)
    )
    return jnp.where(fine, 0.0, NEG_LARGE)


def tall(refs, low, high):
    return jnp.concatenate([ref[:, low:high] for ref in refs], axis=0)


def split_three(values):
    first = values.astype(jnp.bfloat16)
    rest = values - first.astype(jnp.float32)
    second = rest.astype(jnp.bfloat16)
    third = (rest - second.astype(jnp.float32)).astype(jnp.bfloat16)
    return first, second, third


def stream_kernel(
    stream_ref, grad_ref, gain_ref, route_ref, back_ref, att_ref, stats_ref, plain_ref, packed_ref
):
    width = stream_ref.shape[1]
    size = width // HEADS
    gain = gain_ref[...]
    normed, inv_std, _ = layer_norm(stream_ref[...], gain)
    slots = as_column(slot_numbers(route_ref[...])).astype(jnp.int32)
    grad_in = unpack_rows(unpack_tables(slots, back_ref.shape[0]), back_ref[...])
    grad_stream = (
        grad_ref[...].astype(jnp.float32) + norm_backward(grad_in, normed, inv_std, gain)
    ).astype(jnp.bfloat16)
    plain_ref[...] = grad_stream
    packed_ref[:, :width] = grad_stream
    products = grad_stream.astype(jnp.float32) * att_ref[...]
    feature = lax.broadcasted_iota(jnp.int32, (width, 128), 0)
    first = lax.broadcasted_iota(jnp.int32, (width, 128), 1) * size
    owner = jnp.where((feature >= first) & (feature < first + size), 1.0, 0.0).astype(jnp.bfloat16)
    delta = sum(nn_dot(piece, owner) for piece in split_three(products))
    source = lax.broadcasted_iota(jnp.int32, (128, 128), 0)
    target = lax.broadcasted_iota(jnp.int32, (128, 128), 1)
    total = jnp.zeros(delta.shape, jnp.float32)
    pieces = split_three(stats_ref[...]) + split_three(delta)
    for place, piece in enumerate(pieces):
        move = (target == source + place * HEADS) & (source < HEADS)
        total = total + nn_dot(piece, jnp.where(move, 1.0, 0.0).astype(jnp.bfloat16))
    packed_ref[:, width:] = total.astype(jnp.bfloat16)


def backward_kernel(
    sizes,
    left_ref,
    mid_ref,
    right_ref,
    gleft_ref,
    gmid_ref,
    gright_ref,
    gq_ref,
    gk_ref,
    gv_ref,
    bias_ref,
    acc_q,
    acc_k,
    acc_v,
):
    band, cols, rows_total, cols_total = sizes
    width = gq_ref.shape[1]
    size = width // HEADS
    scale = size ** (-0.5)
    tokens = band * cols
    own = slice(RAD * cols, RAD * cols + tokens)
    refs = (left_ref, mid_ref, right_ref)
    grefs = (gleft_ref, gmid_ref, gright_ref)
    bias_ref[...] = window_bias(band, cols, rows_total, cols_total)
    for acc in (acc_q, acc_k, acc_v):
        acc[...] = jnp.zeros_like(acc)
    row = lax.broadcasted_iota(jnp.int32, (2 * HEADS, 128), 0)
    lane = lax.broadcasted_iota(jnp.int32, (2 * HEADS, 128), 1)
    base = jnp.where(row < HEADS, row, row + 2 * HEADS)
    pick = jnp.where(
        (lane == base) | (lane == base + HEADS) | (lane == base + 2 * HEADS), 1.0, 0.0
    ).astype(jnp.bfloat16)
    stats_far = nt_dot(pick, tall(grefs, width, width + 128))
    stats_own = nt_dot(gmid_ref[own, width : width + 128], pick)
    for head in range(HEADS):
        start, low, high = head_lanes(head, size, width)
        mask = lane_mask(head, size, low, high)
        mask_low = mask.astype(jnp.bfloat16)
        keys = tall(refs, low, high)
        values = tall(refs, width + low, width + high)
        queries = tall(refs, 2 * width + low, 2 * width + high)
        grads = tall(grefs, low, high)
        bias = bias_ref[...]
        own_key = mid_ref[own, low:high] * mask_low
        own_value = mid_ref[own, width + low : width + high] * mask_low
        own_query = mid_ref[own, 2 * width + low : 2 * width + high] * mask_low
        own_grad = gmid_ref[own, low:high] * mask_low

        probs = jnp.exp(
            nt_dot(own_query, keys) * scale + bias - stats_own[:, head : head + 1]
        )
        grad_probs = nt_dot(own_grad, values)
        grad_scores = (
            probs * (grad_probs - stats_own[:, HEADS + head : HEADS + head + 1])
        ).astype(jnp.bfloat16)
        acc_q[:, low:high] += jnp.where(mask, nn_dot(grad_scores, keys), 0.0)

        probs = jnp.exp(
            nt_dot(own_key, queries) * scale + bias - stats_far[head : head + 1, :]
        )
        acc_v[:, low:high] += jnp.where(mask, nn_dot(probs.astype(jnp.bfloat16), grads), 0.0)
        grad_probs = nt_dot(own_value, grads)
        grad_scores = (
            probs * (grad_probs - stats_far[HEADS + head : HEADS + head + 1, :])
        ).astype(jnp.bfloat16)
        acc_k[:, low:high] += jnp.where(mask, nn_dot(grad_scores, queries), 0.0)
    gq_ref[...] = (acc_q[...] * scale).astype(jnp.bfloat16)
    gk_ref[...] = (acc_k[...] * scale).astype(jnp.bfloat16)
    gv_ref[...] = acc_v[...].astype(jnp.bfloat16)


def vmem():
    return pl.BlockSpec(memory_space=pltpu.VMEM)


def anywhere():
    return pl.BlockSpec(memory_space=pl.ANY)


def params(collective_id=None):
    if collective_id is None:
        return pltpu.CompilerParams(vmem_limit_bytes=VMEM_LIMIT)
    return pltpu.CompilerParams(
        vmem_limit_bytes=VMEM_LIMIT, collective_id=collective_id, has_side_effects=True
    )


def shaped(shape, kind=jnp.bfloat16):
    return jax.ShapeDtypeStruct(shape, kind)


def body(
    query_act,
    key_act,
    value_act,
    stream,
    grad_out,
    norm_gain,
    route_ids,
    gate_prob,
    weight_in,
    weight_out,
):
    band, cols, width = stream.shape
    tokens = band * cols
    experts = lax.axis_size("dp")
    col_parts = lax.axis_size("expert")
    sizes = (band, cols, band * experts, cols * col_parts)
    side = (band + 2 * RAD) * cols
    dma = pltpu.SemaphoreType.DMA
    flat_query, flat_key, flat_value, flat_stream, flat_grad = (
        array.reshape(tokens, width) for array in (query_act, key_act, value_act, stream, grad_out)
    )
    gain = norm_gain.reshape(1, width)
    routes = route_ids.reshape(1, tokens)
    bf = jnp.bfloat16
    hidden_units = weight_in.shape[-1]
    *near, returned, attended, log_total, grad_first, grad_second = pl.pallas_call(
        functools.partial(expert_kernel, sizes),
        out_shape=(shaped((side, 3 * width)),) * 3
        + (
            shaped((experts, 16, 640)),
            shaped((tokens, width), jnp.float32),
            shaped((tokens, 128), jnp.float32),
            shaped((width, hidden_units)),
            shaped((hidden_units, width)),
        ),
        in_specs=[anywhere()] * 2 + [vmem()] * 3 + [anywhere()] * 5,
        out_specs=(anywhere(),) * 3 + (vmem(),) * 3 + (anywhere(),) * 2,
        scratch_shapes=[
            pltpu.VMEM((tokens, width), bf),
            pltpu.VMEM((tokens, width), bf),
            pltpu.VMEM((width, hidden_units), bf),
            pltpu.VMEM((hidden_units, width), bf),
            pltpu.VMEM((experts * 16, 1280), bf),
            pltpu.VMEM((4, 128, 1280), bf),
            pltpu.VMEM((4, 384, width), bf),
            pltpu.VMEM((4, 384, width), bf),
            pltpu.VMEM((4, 384, hidden_units), bf),
            pltpu.VMEM((4, 384, hidden_units), bf),
            pltpu.VMEM((4, 384, width), bf),
            pltpu.VMEM((4, 4, 48, width), bf),
            pltpu.VMEM((4, 4, 48, width), bf),
            pltpu.VMEM((4, 48, width), bf),
            pltpu.VMEM((4, 48, width), bf),
            pltpu.VMEM((4, 48, width), bf),
            pltpu.VMEM((4, 128, 640), bf),
            pltpu.VMEM((side, 3 * width), bf),
            pltpu.VMEM((side, 3 * width), bf),
            pltpu.VMEM((side, 3 * width), bf),
            pltpu.VMEM((tokens, 3 * side), jnp.float32),
            pltpu.VMEM((width, hidden_units), bf),
            pltpu.VMEM((hidden_units, width), bf),
            dma((4,)),
            dma((2,)),
            dma((3, 8)),
            dma((3, 8)),
            dma((3,)),
            dma((3,)),
            dma((32,)),
            dma((32,)),
            dma,
            dma((4, 2, 7)),
            dma((8, 4, 2)),
            dma((4, 4)),
            dma((4, 4)),
            dma((4,)),
            dma((4,)),
            dma((2, 4)),
            dma((2, 4)),
            dma((32,)),
            dma((32,)),
            dma,
        ],
        compiler_params=params(1),
        name="expert",
    )(
        flat_stream,
        flat_grad,
        gain,
        gate_prob.reshape(1, tokens),
        routes,
        flat_key,
        flat_value,
        flat_query,
        weight_in[0],
        weight_out[0],
    )
    plain, packed = pl.pallas_call(
        stream_kernel,
        out_shape=(shaped((tokens, width)), shaped((tokens, width + 128))),
        in_specs=[vmem()] * 7,
        out_specs=(vmem(), vmem()),
        compiler_params=params(),
        name="stream_grad",
    )(flat_stream, flat_grad, gain, routes, returned.reshape(-1, 640), attended, log_total)
    far = pl.pallas_call(
        halo_kernel,
        out_shape=(shaped((side, width + 128)),) * 3,
        in_specs=[vmem()],
        out_specs=(vmem(),) * 3,
        scratch_shapes=[dma((8,)), dma((8,)), dma],
        compiler_params=params(3),
        name="halo",
    )(packed)
    grad_query, grad_key, grad_value = pl.pallas_call(
        functools.partial(backward_kernel, sizes),
        out_shape=(shaped((tokens, width)),) * 3,
        in_specs=[vmem()] * 6,
        out_specs=(vmem(),) * 3,
        scratch_shapes=[pltpu.VMEM((tokens, 3 * side), jnp.float32)]
        + [pltpu.VMEM((tokens, width), jnp.float32)] * 3,
        compiler_params=params(),
        name="attend_back",
    )(*near, *far)
    shape = (band, cols, width)
    return (
        grad_query.reshape(shape),
        grad_key.reshape(shape),
        grad_value.reshape(shape),
        plain.reshape(shape),
        grad_first[None],
        grad_second[None],
    )


def solution(mesh):
    in_specs = (
        P("dp", "expert", None),
        P("dp", "expert", None),
        P("dp", "expert", None),
        P("dp", "expert", None),
        P("dp", "expert", None),
        P(),
        P("dp", "expert", None, None),
        P("dp", "expert", None),
        P("dp", None, "expert"),
        P("dp", "expert", None),
    )
    out_specs = (
        P("dp", "expert", None),
        P("dp", "expert", None),
        P("dp", "expert", None),
        P("dp", "expert", None),
        P("dp", None, "expert"),
        P("dp", "expert", None),
    )
    return jax.shard_map(body, mesh=mesh, in_specs=in_specs, out_specs=out_specs, check_vma=False)
```

```python
import functools

import jax
import jax.numpy as jnp
from jax import lax
from jax.experimental import pallas as pl
from jax.experimental.pallas import tpu as pltpu
from jax.sharding import PartitionSpec as P

HEADS = 16
RAD = 6
SLOTS = 6
MESH = pl.DeviceIdType.MESH
VMEM_LIMIT = 60 * 1024 * 1024
TAIL_LIMIT = 60 * 1024 * 1024


LN_EPS = 1e-05
ROOT_HALF = 0.7071067811865476
INV_ROOT_TAU = 0.3989422804014327
NEG_LARGE = -1e30


def gelu_value(values):
    return 0.5 * values * (1.0 + lax.erf(values * ROOT_HALF))


def gelu_slope(values):
    return (
        0.5 * (1.0 + lax.erf(values * ROOT_HALF))
        + values * jnp.exp(-0.5 * values * values) * INV_ROOT_TAU
    )


def layer_norm(stream, norm_gain):
    values = stream.astype(jnp.float32)
    center = values - jnp.mean(values, axis=-1, keepdims=True)
    inv_std = lax.rsqrt(jnp.mean(center * center, axis=-1, keepdims=True) + LN_EPS)
    normed = center * inv_std
    return (normed, inv_std, (normed * norm_gain).astype(jnp.bfloat16))


def norm_backward(grad_in, normed, inv_std, norm_gain):
    scaled = grad_in * norm_gain
    centered = scaled - jnp.mean(scaled, axis=-1, keepdims=True)
    return inv_std * (centered - normed * jnp.mean(scaled * normed, axis=-1, keepdims=True))


def unit_places(index, first):
    place = index % 16
    block = index // 16
    rank = place - first
    return jnp.where((rank >= 0) & (rank < SLOTS), block * SLOTS + rank, -1)


def slot_rows(index):
    place = index % 16
    block = index // 16
    tail = jnp.where(place >= 12, block * SLOTS + place - 12, -1)
    late = jnp.where((place == 12) | (place == 13), block * SLOTS + place - 8, -1)
    last = jnp.where(place >= 14, block * SLOTS + place - 10, -1)
    return (unit_places(index, 0), unit_places(index, 6), tail, late, last)


def pack_tables(slots, rows):
    index = lax.broadcasted_iota(jnp.int32, (rows, 1), 0)
    return [jnp.where(held == slots, 1.0, 0.0).astype(jnp.bfloat16) for held in slot_rows(index)]


def unpack_tables(slots, rows):
    index = lax.broadcasted_iota(jnp.int32, (1, rows), 1)
    return [jnp.where(held == slots, 1.0, 0.0).astype(jnp.bfloat16) for held in slot_rows(index)]


def pack_rows(tables, values):
    t0, t1, t2, t3, t4 = tables
    chunk = [values[:, 128 * i : 128 * (i + 1)] for i in range(10, 13)]
    tail = jnp.concatenate(
        [
            nn_dot(t2, values[:, 1280:1664]),
            nn_dot(t3, chunk[0]) + nn_dot(t4, chunk[1]),
            nn_dot(t3, chunk[2]),
        ],
        axis=1,
    )
    return (nn_dot(t0, values[:, :640]) + nn_dot(t1, values[:, 640:1280]) + tail).astype(
        jnp.bfloat16
    )


def unpack_rows(tables, packed):
    t0, t1, t2, t3, t4 = tables
    third, fourth = packed[:, 384:512], packed[:, 512:640]
    extra = jnp.concatenate([nn_dot(t3, third), nn_dot(t4, third), nn_dot(t3, fourth)], axis=1)
    return jnp.concatenate(
        [nn_dot(t0, packed), nn_dot(t1, packed), nn_dot(t2, packed[:, :384]) + extra], axis=1
    )


def as_column(row):
    count = row.shape[1]
    diagonal = lax.broadcasted_iota(jnp.int32, (count, count), 0) == lax.broadcasted_iota(
        jnp.int32, (count, count), 1
    )
    return jnp.sum(jnp.where(diagonal, row, 0.0), axis=1, keepdims=True)


def slot_numbers(routes):
    tokens = routes.shape[1]
    onehot = lax.broadcasted_iota(jnp.int32, (128, tokens), 0) == routes
    onehot = jnp.where(onehot, 1.0, 0.0)
    earlier = lax.broadcasted_iota(jnp.int32, (tokens, tokens), 0) < lax.broadcasted_iota(
        jnp.int32, (tokens, tokens), 1
    )
    before = nn_dot(
        onehot.astype(jnp.bfloat16), jnp.where(earlier, 1.0, 0.0).astype(jnp.bfloat16)
    )
    rank = jnp.sum(before * onehot, axis=0, keepdims=True)
    return routes.astype(jnp.float32) * SLOTS + rank


def write_messages(stream, grad, gain, gate, route, out_ref):
    _, _, expert_in = layer_norm(stream, gain)
    grad_z = (as_column(gate) * grad.astype(jnp.float32)).astype(jnp.bfloat16)
    slots = slot_numbers(route).astype(jnp.int32)
    tables = pack_tables(slots, out_ref.shape[0])
    out_ref[:, :640] = pack_rows(tables, expert_in)
    out_ref[:, 640:] = pack_rows(tables, grad_z)


def ring_places():
    e = lax.axis_index("expert")
    d = lax.axis_index("dp")
    places = dict(
        right=lax.rem(e + 2, 8),
        left=lax.rem(e + 6, 8),
        far=lax.rem(e + 4, 8),
        pair=e + 1 - 2 * lax.rem(e, 2),
        beside=lax.rem(e + 7 + 2 * lax.rem(e, 2), 8),
    )
    return e, d, d // 8, lax.rem(d, 8), places


def around(e, d):
    places = []
    for down, over in ((0, 1), (0, -1), (-1, 0), (1, 0)):
        places.append((down, over, lax.rem(d + 32 + down, 32), lax.rem(e + 8 + over, 8)))
    return places


def greet_all(e, d, places):
    barrier = pltpu.get_barrier_semaphore()

    def greet(i, carry):
        pl.semaphore_signal(
            barrier, inc=1, device_id={"dp": lax.rem(d + i, 32)}, device_id_type=MESH
        )
        return carry

    lax.fori_loop(1, 32, greet, 0)
    for name in ("right", "left", "pair", "beside"):
        pl.semaphore_signal(
            barrier, inc=1, device_id={"expert": places[name]}, device_id_type=MESH
        )
    pl.semaphore_wait(barrier, 35)


def remote(src, dst, send, recv, **where):
    return pltpu.make_async_remote_copy(
        src_ref=src, dst_ref=dst, send_sem=send, recv_sem=recv, device_id=where, device_id_type=MESH
    )


def tn_dot(left, right):
    return lax.dot_general(left, right, (((0,), (0,)), ((), ())), preferred_element_type=jnp.float32)


def rim_slices(down, tokens, rim):
    if down == 0:
        return pl.ds(0, tokens), pl.ds(rim, tokens)
    if down == 1:
        return pl.ds(tokens - rim, rim), pl.ds(0, rim)
    return pl.ds(0, rim), pl.ds(rim + tokens, rim)


def corner_copies(e, d, rim, tokens, left, mid, right, send, recv):
    copies = []
    for _, over, row, col in around(e, d)[:2]:
        for low in (0, rim + tokens):
            number = len(copies)
            copies.append(
                remote(
                    mid.at[pl.ds(low, rim)],
                    (left if over == 1 else right).at[pl.ds(low, rim)],
                    send.at[number],
                    recv.at[number],
                    expert=col,
                )
            )
    return copies


def expert_kernel(
    sizes,
    stream_hbm,
    grad_hbm,
    gain_ref,
    gate_ref,
    route_ref,
    key_hbm,
    value_hbm,
    query_hbm,
    first_hbm,
    second_hbm,
    left_hbm,
    mid_hbm,
    right_hbm,
    out_ref,
    att_ref,
    stats_ref,
    grad_first_hbm,
    grad_second_hbm,
    stream_v,
    grad_v,
    first_v,
    second_v,
    msg,
    recv,
    bx,
    bg,
    hidden,
    grad_pre,
    back,
    from_pair,
    mine,
    from_left,
    from_right,
    early,
    packed,
    left_v,
    mid_v,
    right_v,
    bias_ref,
    grad_first_v,
    grad_second_v,
    first_acc,
    second_acc,
    load_sem,
    store_sem,
    halo_send,
    halo_recv,
    halo_keep,
    halo_out,
    corner_send,
    corner_recv,
    all_send,
    all_recv,
    own_sem,
    ring_send,
    ring_recv,
    pair_send,
    pair_recv,
    far_send,
    far_recv,
    near_send,
    near_recv,
    home_send,
    home_recv,
    home_sem,
):
    e, d, x, z, places = ring_places()
    right, left, far, pair = (places[name] for name in ("right", "left", "far", "pair"))
    tokens, width = stream_hbm.shape
    rim = RAD * sizes[1]
    boxes = (bx, bg)
    sent = []

    loads = [
        pltpu.make_async_copy(source, target, load_sem.at[i])
        for i, (source, target) in enumerate(
            (
                (stream_hbm, stream_v),
                (grad_hbm, grad_v),
                (first_hbm, first_v),
                (second_hbm, second_v),
            )
        )
    ]
    lanes = [pl.ds(i * width, width) for i in range(3)]
    sources = (key_hbm, value_hbm, query_hbm)
    keeps = [
        pltpu.make_async_copy(
            sources[i], mid_v.at[pl.ds(rim, tokens), lanes[i]], halo_keep.at[i]
        )
        for i in range(3)
    ]
    for copy in loads + keeps:
        copy.start()
    greet_all(e, d, places)

    halos = []
    for number, (down, over, row, col) in enumerate(around(e, d)):
        side = {1: left_v, 0: mid_v, -1: right_v}[over]
        src, dst = rim_slices(down, tokens, rim)
        halos.append(
            remote(
                mid_v.at[pl.ds(src.start + rim, src.size)],
                side.at[dst],
                halo_send.at[number],
                halo_recv.at[number],
                dp=row,
                expert=col,
            )
        )
    for copy in keeps:
        copy.wait()
    for copy in halos[:2]:
        copy.start()
    corners = corner_copies(e, d, rim, tokens, left_v, mid_v, right_v, corner_send, corner_recv)

    loads[0].wait()
    loads[1].wait()
    write_messages(stream_v[...], grad_v[...], gain_ref[...].reshape(1, -1), gate_ref[...], route_ref[...], msg)

    def rows16(index):
        return pl.ds(pl.multiple_of(index * 16, 16), 16)

    def rows48(index):
        return pl.ds(pl.multiple_of(index * 48, 16), 48)

    def message(target):
        return remote(
            msg.at[rows16(target)],
            recv.at[x, rows16(z)],
            all_send.at[target],
            all_recv.at[d],
            dp=target,
        )

    own = pltpu.make_async_copy(msg.at[rows16(d)], recv.at[x, rows16(z)], own_sem)
    own.start()
    for g in range(4):
        row = lax.rem(x + g, 4) * 8

        def send(i, carry):
            message(row + lax.rem(z + i, 8)).start()
            return carry

        lax.fori_loop(1 if g == 0 else 0, 8, send, 0)
    for copy in halos[2:]:
        copy.start()

    index = lax.broadcasted_iota(jnp.int32, (8 * SLOTS, 1), 0)
    unpacking = unpack_tables(index, 128)
    index = lax.broadcasted_iota(jnp.int32, (1, 8 * SLOTS), 1)
    packing = pack_tables(index, 128)

    def group(g):
        return lax.rem(x + 4 - g, 4)

    def ring(source, g, kind, where, number):
        block = boxes[kind].at[group(g), rows48(source)]
        return remote(
            block,
            block,
            ring_send.at[g, kind, number],
            ring_recv.at[source, g, kind],
            expert=places[where],
        )

    def go(copy):
        copy.start()
        sent.append(copy)

    def arrive(g):
        row = group(g) * 8

        def take(i, carry):
            source = row + lax.rem(z + 8 - i, 8)
            remote(
                msg.at[rows16(source)],
                recv.at[group(g), rows16(lax.rem(source, 8))],
                all_send.at[source],
                all_recv.at[source],
                dp=source,
            ).wait_recv()
            return carry

        lax.fori_loop(1 if g == 0 else 0, 8, take, 0)
        if g == 0:
            own.wait()
        for kind in range(2):
            got = recv[group(g), :, 640 * kind : 640 * (kind + 1)]
            boxes[kind][group(g), rows48(e), :] = unpack_rows(unpacking, got).astype(jnp.bfloat16)
            for number, where in enumerate(("right", "left", "pair")):
                go(ring(e, g, kind, where, number))

    def relay(g):
        for name, onward, passed, number in (("left", "right", 0, 4), ("right", "left", 1, 5)):
            for kind in range(2):
                ring(places[name], g, kind, "right", 0).wait_recv()
                if kind == passed:
                    go(ring(places[name], g, kind, onward, 3))
                go(ring(places[name], g, kind, "pair", number))

    def finish(g):
        for kind in range(2):
            ring(far, g, kind, "right", 0).wait_recv()
            go(ring(far, g, kind, "pair", 6))

    side_of = lax.rem(e, 2)
    steps = ((2, far), (1, right), (3, left), (0, e))

    def pair_copy(step, target, g):
        return remote(
            back.at[group(g), rows48(target + pair - e)],
            from_pair.at[step, g],
            pair_send.at[step, g],
            pair_recv.at[step, g],
            expert=pair,
        )

    def work(g):
        for y in range(4):
            for kind in range(2):
                ring(2 * y + 1 - side_of, g, kind, "right", 0).wait_recv()
        at = group(g)
        for low in range(0, 512, 256):
            cut = slice(low, low + 256)
            pre_act = nn_dot(bx[at], first_v[:, cut])
            grad_hidden = nt_dot(bg[at], second_v[cut, :])
            hidden[at, :, cut] = gelu_value(pre_act).astype(jnp.bfloat16)
            grad_pre[at, :, cut] = (grad_hidden * gelu_slope(pre_act)).astype(jnp.bfloat16)
        for low in range(0, width, 512):
            cut = slice(low, min(low + 512, width))
            back[at, :, cut] = nt_dot(grad_pre[at], first_v[cut, :]).astype(jnp.bfloat16)
        for step, target in steps:
            go(pair_copy(step, target, g))

    def joined(step, target, g):
        return back[group(g), rows48(target), :].astype(jnp.float32) + from_pair[step, g].astype(
            jnp.float32
        )

    def far_copy(g):
        return remote(
            mine.at[2, g],
            early.at[g],
            far_send.at[g],
            far_recv.at[g],
            expert=left if g % 2 else right,
        )

    def near_copy(step, g):
        return remote(
            mine.at[step, g],
            (from_left if step == 1 else from_right).at[g],
            near_send.at[step // 2, g],
            near_recv.at[step // 2, g],
            expert=right if step == 1 else left,
        )

    def share(g):
        for step, target in steps:
            pair_copy(step, target, g).wait_recv()
        mine[2, g] = joined(2, far, g).astype(jnp.bfloat16)
        go(far_copy(g))
        step, target = (1, right) if g % 2 else (3, left)
        mine[step, g] = joined(step, target, g).astype(jnp.bfloat16)
        go(near_copy(step, g))

    def add_far(g):
        far_copy(g).wait_recv()
        step, target = (3, left) if g % 2 else (1, right)
        mine[step, g] = (joined(step, target, g) + early[g].astype(jnp.float32)).astype(
            jnp.bfloat16
        )
        go(near_copy(step, g))

    def home(g, i):
        place = lax.rem(z + i, 8)
        target = group(g) * 8 + place
        return remote(
            packed.at[g, rows16(place)],
            out_ref.at[d],
            home_send.at[target],
            home_recv.at[d],
            dp=target,
        )

    home_own = pltpu.make_async_copy(packed.at[0, rows16(z)], out_ref.at[d], home_sem)

    def give(g):
        near_copy(1, g).wait_recv()
        near_copy(3, g).wait_recv()
        total = (
            joined(0, e, g) + from_left[g].astype(jnp.float32) + from_right[g].astype(jnp.float32)
        )
        packed[g] = pack_rows(packing, total.astype(jnp.bfloat16))

        def send(i, carry):
            home(g, i).start()
            return carry

        lax.fori_loop(1 if g == 0 else 0, 8, send, 0)
        if g == 0:
            home_own.start()

    outs = [
        pltpu.make_async_copy(source, target, halo_out.at[i])
        for i, (source, target) in enumerate(
            ((left_v, left_hbm), (mid_v, mid_hbm), (right_v, right_hbm))
        )
    ]

    def corner():
        for copy in halos[2:]:
            copy.wait_recv()
        for copy in corners:
            copy.start()

    def look():
        for copy in halos[:2] + corners:
            copy.wait_recv()
        for copy in outs:
            copy.start()
        bias_ref[...] = window_bias(*sizes)
        att_ref[...] = jnp.zeros_like(att_ref)
        stats_ref[...] = jnp.zeros_like(stats_ref)

    def attend(heads):
        own_rows = slice(rim, rim + tokens)
        refs = (left_v, mid_v, right_v)
        size = width // HEADS
        scale = size ** (-0.5)
        lane = lax.broadcasted_iota(jnp.int32, stats_ref.shape, 1)
        stats = stats_ref[...]
        for head in heads:
            start, low, high = head_lanes(head, size, width)
            mask = lane_mask(head, size, low, high)
            queries = mid_v[own_rows, 2 * width + low : 2 * width + high] * mask.astype(
                jnp.bfloat16
            )
            scores = nt_dot(queries, tall(refs, low, high)) * scale + bias_ref[...]
            peak = jnp.max(scores, axis=-1, keepdims=True)
            log_total = peak + jnp.log(jnp.sum(jnp.exp(scores - peak), axis=-1, keepdims=True))
            probs_low = jnp.exp(scores - log_total).astype(jnp.bfloat16)
            attended = nn_dot(probs_low, tall(refs, width + low, width + high))
            att_ref[:, low:high] += jnp.where(mask, attended, 0.0)
            stats = jnp.where(lane == head, log_total, stats)
        stats_ref[...] = stats

    def weight_grads(g):
        at = group(g)
        for lefts, rights, total, final in (
            (bx, grad_pre, first_acc, grad_first_v),
            (hidden, bg, second_acc, grad_second_v),
        ):
            for low in range(0, total.shape[0], 256):
                cut = slice(low, min(low + 256, total.shape[0]))
                part = tn_dot(lefts[at, :, cut], rights[at])
                if g > 0:
                    part = part + total[cut, :]
                if g < 3:
                    total[cut, :] = part
                else:
                    final[cut, :] = part.astype(jnp.bfloat16)

    stores = [
        pltpu.make_async_copy(grad_first_v, grad_first_hbm, store_sem.at[0]),
        pltpu.make_async_copy(grad_second_v, grad_second_hbm, store_sem.at[1]),
    ]

    arrive(0)
    arrive(1)
    relay(0)
    arrive(2)
    finish(0)
    relay(1)
    loads[2].wait()
    loads[3].wait()
    work(0)
    arrive(3)
    corner()
    finish(1)
    relay(2)
    share(0)
    work(1)
    weight_grads(0)
    finish(2)
    relay(3)
    add_far(0)
    share(1)
    work(2)
    look()
    attend(range(0, 6))
    finish(3)
    give(0)
    add_far(1)
    share(2)
    work(3)
    share(3)
    attend(range(6, 10))
    give(1)
    add_far(2)
    attend(range(10, 16))
    add_far(3)
    give(2)
    weight_grads(1)
    give(3)
    weight_grads(2)
    weight_grads(3)
    for copy in stores:
        copy.start()

    def take_home(i, carry):
        source = lax.rem(d + i, 32)
        remote(
            packed.at[0, pl.ds(0, 16)],
            out_ref.at[source],
            home_send.at[source],
            home_recv.at[source],
            dp=source,
        ).wait_recv()
        return carry

    lax.fori_loop(1, 32, take_home, 0)
    home_own.wait()
    for copy in sent + halos + corners:
        copy.wait_send()

    def sent_all(i, carry):
        message(lax.rem(d + i, 32)).wait_send()
        return carry

    lax.fori_loop(1, 32, sent_all, 0)
    for g in range(4):

        def sent_home(i, carry):
            home(g, i).wait_send()
            return carry

        lax.fori_loop(1 if g == 0 else 0, 8, sent_home, 0)
    for copy in outs + stores:
        copy.wait()


def head_lanes(head, size, width):
    start = head * size
    low = start // 128 * 128
    high = min((start + size + 127) // 128 * 128, width)
    return start, low, high


def lane_mask(head, size, low, high):
    lanes = lax.broadcasted_iota(jnp.int32, (1, high - low), 1) + low
    return (lanes >= head * size) & (lanes < (head + 1) * size)


def nt_dot(left, right):
    return lax.dot_general(left, right, (((1,), (1,)), ((), ())), preferred_element_type=jnp.float32)


def nn_dot(left, right):
    return jnp.dot(left, right, preferred_element_type=jnp.float32)


def window_bias(band, cols, rows_total, cols_total):
    row_index = lax.axis_index("dp")
    col_index = lax.axis_index("expert")
    side = (band + 2 * RAD) * cols
    shape = (band * cols, 3 * side)
    shift = cols.bit_length() - 1
    own = lax.broadcasted_iota(jnp.int32, shape, 0)
    far = lax.broadcasted_iota(jnp.int32, shape, 1)
    part = (far >= side).astype(jnp.int32) + (far >= 2 * side).astype(jnp.int32)
    within = far - side * part
    far_row = (within >> shift) - RAD
    far_col = (within & (cols - 1)) + cols * (part - 1)
    own_row = own >> shift
    own_col = own & (cols - 1)
    abs_row = far_row + row_index * band
    abs_col = far_col + col_index * cols
    fine = (
        (jnp.abs(far_row - own_row) <= RAD)
        & (jnp.abs(far_col - own_col) <= RAD)
        & (abs_row >= 0)
        & (abs_row < rows_total)
        & (abs_col >= 0)
        & (abs_col < cols_total)
    )
    return jnp.where(fine, 0.0, NEG_LARGE)


def tall(refs, low, high):
    return jnp.concatenate([ref[:, low:high] for ref in refs], axis=0)


def split_three(values):
    first = values.astype(jnp.bfloat16)
    rest = values - first.astype(jnp.float32)
    second = rest.astype(jnp.bfloat16)
    third = (rest - second.astype(jnp.float32)).astype(jnp.bfloat16)
    return first, second, third


def stream_grad(stream, grad, gain, route, back, attended, log_total):
    width = stream.shape[1]
    size = width // HEADS
    normed, inv_std, _ = layer_norm(stream, gain)
    slots = as_column(slot_numbers(route)).astype(jnp.int32)
    grad_in = unpack_rows(unpack_tables(slots, back.shape[0]), back)
    grad_stream = (
        grad.astype(jnp.float32) + norm_backward(grad_in, normed, inv_std, gain)
    ).astype(jnp.bfloat16)
    products = grad_stream.astype(jnp.float32) * attended
    feature = lax.broadcasted_iota(jnp.int32, (width, 128), 0)
    first = lax.broadcasted_iota(jnp.int32, (width, 128), 1) * size
    owner = jnp.where((feature >= first) & (feature < first + size), 1.0, 0.0).astype(jnp.bfloat16)
    delta = sum(nn_dot(piece, owner) for piece in split_three(products))
    source = lax.broadcasted_iota(jnp.int32, (128, 128), 0)
    target = lax.broadcasted_iota(jnp.int32, (128, 128), 1)
    total = jnp.zeros(delta.shape, jnp.float32)
    pieces = split_three(log_total) + split_three(delta)
    for place, piece in enumerate(pieces):
        move = (target == source + place * HEADS) & (source < HEADS)
        total = total + nn_dot(piece, jnp.where(move, 1.0, 0.0).astype(jnp.bfloat16))
    return grad_stream, total.astype(jnp.bfloat16)


def stats_table():
    row = lax.broadcasted_iota(jnp.int32, (2 * HEADS, 128), 0)
    lane = lax.broadcasted_iota(jnp.int32, (2 * HEADS, 128), 1)
    base = jnp.where(row < HEADS, row, row + 2 * HEADS)
    return jnp.where(
        (lane == base) | (lane == base + HEADS) | (lane == base + 2 * HEADS), 1.0, 0.0
    ).astype(jnp.bfloat16)


def turn_kernel(
    sizes,
    stream_hbm,
    grad_hbm,
    gain_ref,
    route_ref,
    back_ref,
    att_ref,
    stats_ref,
    left_hbm,
    mid_hbm,
    right_hbm,
    gleft_ref,
    gmid_ref,
    gright_ref,
    gq_ref,
    stream_v,
    grad_v,
    left_v,
    mid_v,
    right_v,
    query_v,
    bias_ref,
    acc_ref,
    load_sem,
    halo_send,
    halo_recv,
    corner_send,
    corner_recv,
):
    e = lax.axis_index("expert")
    d = lax.axis_index("dp")
    tokens, width = stream_hbm.shape
    size = width // HEADS
    scale = size ** (-0.5)
    rim = RAD * sizes[1]
    own = slice(rim, rim + tokens)
    both = pl.ds(0, 2 * width)
    loads = [
        pltpu.make_async_copy(source, target, load_sem.at[i])
        for i, (source, target) in enumerate(
            (
                (stream_hbm, stream_v),
                (grad_hbm, grad_v),
                (left_hbm.at[:, both], left_v),
                (mid_hbm.at[:, both], mid_v),
                (right_hbm.at[:, both], right_v),
                (mid_hbm.at[pl.ds(rim, tokens), pl.ds(2 * width, width)], query_v),
            )
        )
    ]
    for copy in loads:
        copy.start()
    barrier = pltpu.get_barrier_semaphore()
    for _, _, row, col in around(e, d):
        pl.semaphore_signal(
            barrier, inc=1, device_id={"dp": row, "expert": col}, device_id_type=MESH
        )
    pl.semaphore_wait(barrier, 4)
    loads[0].wait()
    loads[1].wait()
    plain, extra = stream_grad(
        stream_v[...],
        grad_v[...],
        gain_ref[...].reshape(1, -1),
        route_ref[...],
        back_ref[...],
        att_ref[...],
        stats_ref[...],
    )
    gmid_ref[own, :width] = plain
    gmid_ref[own, width:] = extra
    halos = []
    for number, (down, over, row, col) in enumerate(around(e, d)):
        side = {1: gleft_ref, 0: gmid_ref, -1: gright_ref}[over]
        src, dst = rim_slices(down, tokens, rim)
        src = pl.ds(src.start + rim, src.size)
        halos.append(
            remote(
                gmid_ref.at[src],
                side.at[dst],
                halo_send.at[number],
                halo_recv.at[number],
                dp=row,
                expert=col,
            )
        )
    for number in (2, 3, 0, 1):
        halos[number].start()
    corners = corner_copies(
        e, d, rim, tokens, gleft_ref, gmid_ref, gright_ref, corner_send, corner_recv
    )
    bias_ref[...] = window_bias(*sizes)
    acc_ref[...] = jnp.zeros_like(acc_ref)
    stats_own = nt_dot(gmid_ref[own, width : width + 128], stats_table())
    for copy in loads[2:]:
        copy.wait()
    refs = (left_v, mid_v, right_v)
    for head in range(HEADS):
        if head == 5:
            for copy in halos[2:]:
                copy.wait_recv()
            for copy in corners:
                copy.start()
        start, low, high = head_lanes(head, size, width)
        mask = lane_mask(head, size, low, high)
        mask_low = mask.astype(jnp.bfloat16)
        keys = tall(refs, low, high)
        values = tall(refs, width + low, width + high)
        probs = jnp.exp(
            nt_dot(query_v[:, low:high] * mask_low, keys) * scale
            + bias_ref[...]
            - stats_own[:, head : head + 1]
        )
        grad_probs = nt_dot(gmid_ref[own, low:high] * mask_low, values)
        grad_scores = (
            probs * (grad_probs - stats_own[:, HEADS + head : HEADS + head + 1])
        ).astype(jnp.bfloat16)
        acc_ref[:, low:high] += jnp.where(mask, nn_dot(grad_scores, keys), 0.0)
    gq_ref[...] = (acc_ref[...] * scale).astype(jnp.bfloat16)
    for copy in halos[:2] + corners:
        copy.wait_recv()
    for copy in halos + corners:
        copy.wait_send()


def last_kernel(
    sizes,
    left_hbm,
    mid_hbm,
    right_hbm,
    gleft_ref,
    gmid_ref,
    gright_ref,
    gq_hbm,
    first_hbm,
    second_hbm,
    gq_out,
    gk_ref,
    gv_ref,
    plain_ref,
    first_out,
    second_out,
    left_v,
    mid_v,
    right_v,
    own_v,
    bias_ref,
    acc_k,
    acc_v,
    first_v,
    second_v,
    gq_v,
    load_sem,
    pass_sem,
):
    tokens, width = gk_ref.shape
    size = width // HEADS
    scale = size ** (-0.5)
    rim = RAD * sizes[1]
    own = slice(rim, rim + tokens)
    third = pl.ds(2 * width, width)
    loads = [
        pltpu.make_async_copy(source, target, load_sem.at[i])
        for i, (source, target) in enumerate(
            (
                (left_hbm.at[:, third], left_v),
                (mid_hbm.at[:, third], mid_v),
                (right_hbm.at[:, third], right_v),
                (mid_hbm.at[pl.ds(rim, tokens), pl.ds(0, 2 * width)], own_v),
            )
        )
    ]
    fetched = [
        pltpu.make_async_copy(source, target, pass_sem.at[i])
        for i, (source, target) in enumerate(
            ((first_hbm, first_v), (second_hbm, second_v), (gq_hbm, gq_v))
        )
    ]
    passed = [
        pltpu.make_async_copy(source, target, pass_sem.at[i])
        for i, (source, target) in enumerate(
            ((first_v, first_out), (second_v, second_out), (gq_v, gq_out))
        )
    ]
    for copy in loads + fetched:
        copy.start()
    plain_ref[...] = gmid_ref[own, :width]
    bias_ref[...] = window_bias(*sizes)
    acc_k[...] = jnp.zeros_like(acc_k)
    acc_v[...] = jnp.zeros_like(acc_v)
    refs = (left_v, mid_v, right_v)
    grefs = (gleft_ref, gmid_ref, gright_ref)
    stats_far = nt_dot(stats_table(), tall(grefs, width, width + 128))
    for copy in loads:
        copy.wait()
    for head in range(HEADS):
        if head == 4:
            for before, after in zip(fetched, passed):
                before.wait()
                after.start()
        start, low, high = head_lanes(head, size, width)
        mask = lane_mask(head, size, low, high)
        mask_low = mask.astype(jnp.bfloat16)
        queries = tall(refs, low, high)
        grads = tall(grefs, low, high)
        probs = jnp.exp(
            nt_dot(own_v[:, low:high] * mask_low, queries) * scale
            + bias_ref[...]
            - stats_far[head : head + 1, :]
        )
        acc_v[:, low:high] += jnp.where(mask, nn_dot(probs.astype(jnp.bfloat16), grads), 0.0)
        grad_probs = nt_dot(own_v[:, width + low : width + high] * mask_low, grads)
        grad_scores = (
            probs * (grad_probs - stats_far[HEADS + head : HEADS + head + 1, :])
        ).astype(jnp.bfloat16)
        acc_k[:, low:high] += jnp.where(mask, nn_dot(grad_scores, queries), 0.0)
    gk_ref[...] = (acc_k[...] * scale).astype(jnp.bfloat16)
    gv_ref[...] = acc_v[...].astype(jnp.bfloat16)
    for copy in passed:
        copy.wait()


def vmem():
    return pl.BlockSpec(memory_space=pltpu.VMEM)


def anywhere():
    return pl.BlockSpec(memory_space=pl.ANY)


def params(collective_id):
    limit = VMEM_LIMIT if collective_id == 1 else TAIL_LIMIT
    return pltpu.CompilerParams(
        vmem_limit_bytes=limit, collective_id=collective_id, has_side_effects=True
    )


def shaped(shape, kind=jnp.bfloat16):
    return jax.ShapeDtypeStruct(shape, kind)


def body(
    query_act,
    key_act,
    value_act,
    stream,
    grad_out,
    norm_gain,
    route_ids,
    gate_prob,
    weight_in,
    weight_out,
):
    band, cols, width = stream.shape
    tokens = band * cols
    experts = lax.axis_size("dp")
    col_parts = lax.axis_size("expert")
    sizes = (band, cols, band * experts, cols * col_parts)
    side = (band + 2 * RAD) * cols
    dma = pltpu.SemaphoreType.DMA
    flat_query, flat_key, flat_value, flat_stream, flat_grad = (
        array.reshape(tokens, width) for array in (query_act, key_act, value_act, stream, grad_out)
    )
    gain = norm_gain
    routes = route_ids.reshape(1, tokens)
    bf = jnp.bfloat16
    hidden_units = weight_in.shape[-1]
    *near, returned, attended, log_total, grad_first, grad_second = pl.pallas_call(
        functools.partial(expert_kernel, sizes),
        out_shape=(shaped((side, 3 * width)),) * 3
        + (
            shaped((experts, 16, 640)),
            shaped((tokens, width), jnp.float32),
            shaped((tokens, 128), jnp.float32),
            shaped((width, hidden_units)),
            shaped((hidden_units, width)),
        ),
        in_specs=[anywhere()] * 2 + [vmem()] * 3 + [anywhere()] * 5,
        out_specs=(anywhere(),) * 3 + (vmem(),) * 3 + (anywhere(),) * 2,
        scratch_shapes=[
            pltpu.VMEM((tokens, width), bf),
            pltpu.VMEM((tokens, width), bf),
            pltpu.VMEM((width, hidden_units), bf),
            pltpu.VMEM((hidden_units, width), bf),
            pltpu.VMEM((experts * 16, 1280), bf),
            pltpu.VMEM((4, 128, 1280), bf),
            pltpu.VMEM((4, 384, width), bf),
            pltpu.VMEM((4, 384, width), bf),
            pltpu.VMEM((4, 384, hidden_units), bf),
            pltpu.VMEM((4, 384, hidden_units), bf),
            pltpu.VMEM((4, 384, width), bf),
            pltpu.VMEM((4, 4, 48, width), bf),
            pltpu.VMEM((4, 4, 48, width), bf),
            pltpu.VMEM((4, 48, width), bf),
            pltpu.VMEM((4, 48, width), bf),
            pltpu.VMEM((4, 48, width), bf),
            pltpu.VMEM((4, 128, 640), bf),
            pltpu.VMEM((side, 3 * width), bf),
            pltpu.VMEM((side, 3 * width), bf),
            pltpu.VMEM((side, 3 * width), bf),
            pltpu.VMEM((tokens, 3 * side), jnp.float32),
            pltpu.VMEM((width, hidden_units), bf),
            pltpu.VMEM((hidden_units, width), bf),
            pltpu.VMEM((width, hidden_units), jnp.float32),
            pltpu.VMEM((hidden_units, width), jnp.float32),
            dma((4,)),
            dma((2,)),
            dma((4,)),
            dma((4,)),
            dma((3,)),
            dma((3,)),
            dma((4,)),
            dma((4,)),
            dma((32,)),
            dma((32,)),
            dma,
            dma((4, 2, 7)),
            dma((8, 4, 2)),
            dma((4, 4)),
            dma((4, 4)),
            dma((4,)),
            dma((4,)),
            dma((2, 4)),
            dma((2, 4)),
            dma((32,)),
            dma((32,)),
            dma,
        ],
        compiler_params=params(1),
        name="expert",
    )(
        flat_stream,
        flat_grad,
        gain,
        gate_prob.reshape(1, tokens),
        routes,
        flat_key,
        flat_value,
        flat_query,
        weight_in[0],
        weight_out[0],
    )
    gleft, gmid, gright, grad_query = pl.pallas_call(
        functools.partial(turn_kernel, sizes),
        out_shape=(shaped((side, width + 128)),) * 3 + (shaped((tokens, width)),),
        in_specs=[anywhere()] * 2 + [vmem()] * 5 + [anywhere()] * 3,
        out_specs=(vmem(),) * 4,
        scratch_shapes=[
            pltpu.VMEM((tokens, width), bf),
            pltpu.VMEM((tokens, width), bf),
            pltpu.VMEM((side, 2 * width), bf),
            pltpu.VMEM((side, 2 * width), bf),
            pltpu.VMEM((side, 2 * width), bf),
            pltpu.VMEM((tokens, width), bf),
            pltpu.VMEM((tokens, 3 * side), jnp.float32),
            pltpu.VMEM((tokens, width), jnp.float32),
            dma((6,)),
            dma((4,)),
            dma((4,)),
            dma((4,)),
            dma((4,)),
        ],
        compiler_params=params(2),
        name="turn",
    )(
        flat_stream,
        flat_grad,
        gain,
        routes,
        returned.reshape(-1, 640),
        attended,
        log_total,
        *near,
    )
    grad_query, grad_key, grad_value, plain, grad_first, grad_second = pl.pallas_call(
        functools.partial(last_kernel, sizes),
        out_shape=(shaped((tokens, width)),) * 4
        + (shaped((width, hidden_units)), shaped((hidden_units, width))),
        in_specs=[anywhere()] * 3 + [vmem()] * 3 + [anywhere()] * 3,
        out_specs=(anywhere(),) + (vmem(),) * 3 + (anywhere(),) * 2,
        scratch_shapes=[
            pltpu.VMEM((side, width), bf),
            pltpu.VMEM((side, width), bf),
            pltpu.VMEM((side, width), bf),
            pltpu.VMEM((tokens, 2 * width), bf),
            pltpu.VMEM((tokens, 3 * side), jnp.float32),
            pltpu.VMEM((tokens, width), jnp.float32),
            pltpu.VMEM((tokens, width), jnp.float32),
            pltpu.VMEM((width, hidden_units), bf),
            pltpu.VMEM((hidden_units, width), bf),
            pltpu.VMEM((tokens, width), bf),
            dma((4,)),
            dma((3,)),
        ],
        compiler_params=pltpu.CompilerParams(vmem_limit_bytes=TAIL_LIMIT),
        name="last",
    )(*near, gleft, gmid, gright, grad_query, grad_first, grad_second)
    shape = (band, cols, width)
    return (
        grad_query.reshape(shape),
        grad_key.reshape(shape),
        grad_value.reshape(shape),
        plain.reshape(shape),
        grad_first[None],
        grad_second[None],
    )


def solution(mesh):
    in_specs = (
        P("dp", "expert", None),
        P("dp", "expert", None),
        P("dp", "expert", None),
        P("dp", "expert", None),
        P("dp", "expert", None),
        P(),
        P("dp", "expert", None, None),
        P("dp", "expert", None),
        P("dp", None, "expert"),
        P("dp", "expert", None),
    )
    out_specs = (
        P("dp", "expert", None),
        P("dp", "expert", None),
        P("dp", "expert", None),
        P("dp", "expert", None),
        P("dp", None, "expert"),
        P("dp", "expert", None),
    )
    return jax.shard_map(body, mesh=mesh, in_specs=in_specs, out_specs=out_specs, check_vma=False)
```

```python
import functools

import jax
import jax.numpy as jnp
from jax import lax
from jax.experimental import pallas as pl
from jax.experimental.pallas import tpu as pltpu
from jax.sharding import PartitionSpec as P

HEADS = 16
RAD = 6
SLOTS = 6
MESH = pl.DeviceIdType.MESH
VMEM_LIMIT = 60 * 1024 * 1024
TAIL_LIMIT = 60 * 1024 * 1024


LN_EPS = 1e-05
ROOT_HALF = 0.7071067811865476
INV_ROOT_TAU = 0.3989422804014327
NEG_LARGE = -1e30


def gelu_value(values):
    return 0.5 * values * (1.0 + lax.erf(values * ROOT_HALF))


def gelu_slope(values):
    return (
        0.5 * (1.0 + lax.erf(values * ROOT_HALF))
        + values * jnp.exp(-0.5 * values * values) * INV_ROOT_TAU
    )


def layer_norm(stream, norm_gain):
    values = stream.astype(jnp.float32)
    center = values - jnp.mean(values, axis=-1, keepdims=True)
    inv_std = lax.rsqrt(jnp.mean(center * center, axis=-1, keepdims=True) + LN_EPS)
    normed = center * inv_std
    return (normed, inv_std, (normed * norm_gain).astype(jnp.bfloat16))


def norm_backward(grad_in, normed, inv_std, norm_gain):
    scaled = grad_in * norm_gain
    centered = scaled - jnp.mean(scaled, axis=-1, keepdims=True)
    return inv_std * (centered - normed * jnp.mean(scaled * normed, axis=-1, keepdims=True))


def unit_places(index, first):
    place = index % 16
    block = index // 16
    rank = place - first
    return jnp.where((rank >= 0) & (rank < SLOTS), block * SLOTS + rank, -1)


def slot_rows(index):
    place = index % 16
    block = index // 16
    tail = jnp.where(place >= 12, block * SLOTS + place - 12, -1)
    late = jnp.where((place == 12) | (place == 13), block * SLOTS + place - 8, -1)
    last = jnp.where(place >= 14, block * SLOTS + place - 10, -1)
    return (unit_places(index, 0), unit_places(index, 6), tail, late, last)


def pack_tables(slots, rows):
    index = lax.broadcasted_iota(jnp.int32, (rows, 1), 0)
    return [jnp.where(held == slots, 1.0, 0.0).astype(jnp.bfloat16) for held in slot_rows(index)]


def unpack_tables(slots, rows):
    index = lax.broadcasted_iota(jnp.int32, (1, rows), 1)
    return [jnp.where(held == slots, 1.0, 0.0).astype(jnp.bfloat16) for held in slot_rows(index)]


def pack_rows(tables, values):
    t0, t1, t2, t3, t4 = tables
    chunk = [values[:, 128 * i : 128 * (i + 1)] for i in range(10, 13)]
    tail = jnp.concatenate(
        [
            nn_dot(t2, values[:, 1280:1664]),
            nn_dot(t3, chunk[0]) + nn_dot(t4, chunk[1]),
            nn_dot(t3, chunk[2]),
        ],
        axis=1,
    )
    return (nn_dot(t0, values[:, :640]) + nn_dot(t1, values[:, 640:1280]) + tail).astype(
        jnp.bfloat16
    )


def unpack_rows(tables, packed):
    t0, t1, t2, t3, t4 = tables
    third, fourth = packed[:, 384:512], packed[:, 512:640]
    extra = jnp.concatenate([nn_dot(t3, third), nn_dot(t4, third), nn_dot(t3, fourth)], axis=1)
    return jnp.concatenate(
        [nn_dot(t0, packed), nn_dot(t1, packed), nn_dot(t2, packed[:, :384]) + extra], axis=1
    )


def as_column(row):
    count = row.shape[1]
    diagonal = lax.broadcasted_iota(jnp.int32, (count, count), 0) == lax.broadcasted_iota(
        jnp.int32, (count, count), 1
    )
    return jnp.sum(jnp.where(diagonal, row, 0.0), axis=1, keepdims=True)


def slot_numbers(routes):
    tokens = routes.shape[1]
    onehot = lax.broadcasted_iota(jnp.int32, (128, tokens), 0) == routes
    onehot = jnp.where(onehot, 1.0, 0.0)
    earlier = lax.broadcasted_iota(jnp.int32, (tokens, tokens), 0) < lax.broadcasted_iota(
        jnp.int32, (tokens, tokens), 1
    )
    before = nn_dot(
        onehot.astype(jnp.bfloat16), jnp.where(earlier, 1.0, 0.0).astype(jnp.bfloat16)
    )
    rank = jnp.sum(before * onehot, axis=0, keepdims=True)
    return routes.astype(jnp.float32) * SLOTS + rank


def write_messages(stream, grad, gain, gate, route, out_ref):
    _, _, expert_in = layer_norm(stream, gain)
    grad_z = (as_column(gate) * grad.astype(jnp.float32)).astype(jnp.bfloat16)
    slots = slot_numbers(route).astype(jnp.int32)
    tables = pack_tables(slots, out_ref.shape[0])
    out_ref[:, :640] = pack_rows(tables, expert_in)
    out_ref[:, 640:] = pack_rows(tables, grad_z)


def ring_places():
    e = lax.axis_index("expert")
    d = lax.axis_index("dp")
    places = dict(
        right=lax.rem(e + 2, 8),
        left=lax.rem(e + 6, 8),
        far=lax.rem(e + 4, 8),
        pair=e + 1 - 2 * lax.rem(e, 2),
        beside=lax.rem(e + 7 + 2 * lax.rem(e, 2), 8),
    )
    return e, d, d // 8, lax.rem(d, 8), places


def around(e, d):
    places = []
    for down, over in ((0, 1), (0, -1), (-1, 0), (1, 0)):
        places.append((down, over, lax.rem(d + 32 + down, 32), lax.rem(e + 8 + over, 8)))
    return places


def greet_all(e, d, places):
    barrier = pltpu.get_barrier_semaphore()

    def greet(i, carry):
        pl.semaphore_signal(
            barrier, inc=1, device_id={"dp": lax.rem(d + i, 32)}, device_id_type=MESH
        )
        return carry

    lax.fori_loop(1, 32, greet, 0)
    for name in ("right", "left", "pair", "beside"):
        pl.semaphore_signal(
            barrier, inc=1, device_id={"expert": places[name]}, device_id_type=MESH
        )
    return barrier


def remote(src, dst, send, recv, **where):
    return pltpu.make_async_remote_copy(
        src_ref=src, dst_ref=dst, send_sem=send, recv_sem=recv, device_id=where, device_id_type=MESH
    )


def tn_dot(left, right):
    return lax.dot_general(left, right, (((0,), (0,)), ((), ())), preferred_element_type=jnp.float32)


def rim_slices(down, tokens, rim):
    if down == 0:
        return pl.ds(0, tokens), pl.ds(rim, tokens)
    if down == 1:
        return pl.ds(tokens - rim, rim), pl.ds(0, rim)
    return pl.ds(0, rim), pl.ds(rim + tokens, rim)


def corner_copies(e, d, rim, tokens, left, mid, right, send, recv):
    copies = []
    for _, over, row, col in around(e, d)[:2]:
        for low in (0, rim + tokens):
            number = len(copies)
            copies.append(
                remote(
                    mid.at[pl.ds(low, rim)],
                    (left if over == 1 else right).at[pl.ds(low, rim)],
                    send.at[number],
                    recv.at[number],
                    expert=col,
                )
            )
    return copies


def expert_kernel(
    sizes,
    stream_hbm,
    grad_hbm,
    gain_ref,
    gate_ref,
    route_ref,
    key_hbm,
    value_hbm,
    query_hbm,
    first_hbm,
    second_hbm,
    left_hbm,
    mid_hbm,
    right_hbm,
    out_ref,
    att_ref,
    stats_ref,
    grad_first_hbm,
    grad_second_hbm,
    stream_v,
    grad_v,
    first_v,
    second_v,
    msg,
    recv,
    bx,
    bg,
    hidden,
    grad_pre,
    back,
    from_pair,
    mine,
    from_left,
    from_right,
    early,
    packed,
    left_v,
    mid_v,
    right_v,
    bias_ref,
    grad_first_v,
    grad_second_v,
    first_acc,
    second_acc,
    load_sem,
    store_sem,
    halo_send,
    halo_recv,
    halo_keep,
    halo_out,
    corner_send,
    corner_recv,
    all_send,
    all_recv,
    own_sem,
    ring_send,
    ring_recv,
    pair_send,
    pair_recv,
    far_send,
    far_recv,
    near_send,
    near_recv,
    home_send,
    home_recv,
    home_sem,
):
    e, d, x, z, places = ring_places()
    right, left, far, pair = (places[name] for name in ("right", "left", "far", "pair"))
    tokens, width = stream_hbm.shape
    rim = RAD * sizes[1]
    boxes = (bx, bg)
    sent = []

    loads = [
        pltpu.make_async_copy(source, target, load_sem.at[i])
        for i, (source, target) in enumerate(
            (
                (stream_hbm, stream_v),
                (grad_hbm, grad_v),
                (first_hbm, first_v),
                (second_hbm, second_v),
            )
        )
    ]
    lanes = [pl.ds(i * width, width) for i in range(3)]
    sources = (key_hbm, value_hbm, query_hbm)
    keeps = [
        pltpu.make_async_copy(
            sources[i], mid_v.at[pl.ds(rim, tokens), lanes[i]], halo_keep.at[i]
        )
        for i in range(3)
    ]
    for copy in loads[:2] + keeps:
        copy.start()
    barrier = greet_all(e, d, places)
    loads[0].wait()
    loads[1].wait()
    for copy in loads[2:]:
        copy.start()
    write_messages(
        stream_v[...],
        grad_v[...],
        gain_ref[...].reshape(1, -1),
        gate_ref[...],
        route_ref[...],
        msg,
    )
    pl.semaphore_wait(barrier, 35)

    halos = []
    for number, (down, over, row, col) in enumerate(around(e, d)):
        side = {1: left_v, 0: mid_v, -1: right_v}[over]
        src, dst = rim_slices(down, tokens, rim)
        halos.append(
            remote(
                mid_v.at[pl.ds(src.start + rim, src.size)],
                side.at[dst],
                halo_send.at[number],
                halo_recv.at[number],
                dp=row,
                expert=col,
            )
        )
    for copy in keeps:
        copy.wait()
    for copy in halos[:2]:
        copy.start()
    corners = corner_copies(e, d, rim, tokens, left_v, mid_v, right_v, corner_send, corner_recv)

    def rows16(index):
        return pl.ds(pl.multiple_of(index * 16, 16), 16)

    def rows48(index):
        return pl.ds(pl.multiple_of(index * 48, 16), 48)

    def message(target):
        return remote(
            msg.at[rows16(target)],
            recv.at[x, rows16(z)],
            all_send.at[target],
            all_recv.at[d],
            dp=target,
        )

    own = pltpu.make_async_copy(msg.at[rows16(d)], recv.at[x, rows16(z)], own_sem)
    own.start()
    for g in range(4):
        row = lax.rem(x + g, 4) * 8

        def send(i, carry):
            message(row + lax.rem(z + i, 8)).start()
            return carry

        lax.fori_loop(1 if g == 0 else 0, 8, send, 0)
    for copy in halos[2:]:
        copy.start()

    index = lax.broadcasted_iota(jnp.int32, (8 * SLOTS, 1), 0)
    unpacking = unpack_tables(index, 128)
    index = lax.broadcasted_iota(jnp.int32, (1, 8 * SLOTS), 1)
    packing = pack_tables(index, 128)

    def group(g):
        return lax.rem(x + 4 - g, 4)

    def ring(source, g, kind, where, number):
        block = boxes[kind].at[group(g), rows48(source)]
        return remote(
            block,
            block,
            ring_send.at[g, kind, number],
            ring_recv.at[source, g, kind],
            expert=places[where],
        )

    def go(copy):
        copy.start()
        sent.append(copy)

    def arrive(g):
        row = group(g) * 8

        def take(i, carry):
            source = row + lax.rem(z + 8 - i, 8)
            remote(
                msg.at[rows16(source)],
                recv.at[group(g), rows16(lax.rem(source, 8))],
                all_send.at[source],
                all_recv.at[source],
                dp=source,
            ).wait_recv()
            return carry

        lax.fori_loop(1 if g == 0 else 0, 8, take, 0)
        if g == 0:
            own.wait()
        for kind in range(2):
            got = recv[group(g), :, 640 * kind : 640 * (kind + 1)]
            boxes[kind][group(g), rows48(e), :] = unpack_rows(unpacking, got).astype(jnp.bfloat16)
            for number, where in enumerate(("right", "left", "pair")):
                go(ring(e, g, kind, where, number))

    def relay(g):
        for name, onward, passed, number in (("left", "right", 0, 4), ("right", "left", 1, 5)):
            for kind in range(2):
                ring(places[name], g, kind, "right", 0).wait_recv()
                if kind == passed:
                    go(ring(places[name], g, kind, onward, 3))
                go(ring(places[name], g, kind, "pair", number))

    def finish(g):
        for kind in range(2):
            ring(far, g, kind, "right", 0).wait_recv()
            go(ring(far, g, kind, "pair", 6))

    side_of = lax.rem(e, 2)
    steps = ((2, far), (1, right), (3, left), (0, e))

    def pair_copy(step, target, g):
        return remote(
            back.at[group(g), rows48(target + pair - e)],
            from_pair.at[step, g],
            pair_send.at[step, g],
            pair_recv.at[step, g],
            expert=pair,
        )

    def work(g):
        for y in range(4):
            for kind in range(2):
                ring(2 * y + 1 - side_of, g, kind, "right", 0).wait_recv()
        at = group(g)
        for low in range(0, 512, 256):
            cut = slice(low, low + 256)
            pre_act = nn_dot(bx[at], first_v[:, cut])
            grad_hidden = nt_dot(bg[at], second_v[cut, :])
            hidden[at, :, cut] = gelu_value(pre_act).astype(jnp.bfloat16)
            grad_pre[at, :, cut] = (grad_hidden * gelu_slope(pre_act)).astype(jnp.bfloat16)
        for low in range(0, width, 512):
            cut = slice(low, min(low + 512, width))
            back[at, :, cut] = nt_dot(grad_pre[at], first_v[cut, :]).astype(jnp.bfloat16)
        for step, target in steps:
            go(pair_copy(step, target, g))

    def joined(step, target, g):
        return back[group(g), rows48(target), :].astype(jnp.float32) + from_pair[step, g].astype(
            jnp.float32
        )

    def far_copy(g):
        return remote(
            mine.at[2, g],
            early.at[g],
            far_send.at[g],
            far_recv.at[g],
            expert=left if g % 2 else right,
        )

    def near_copy(step, g):
        return remote(
            mine.at[step, g],
            (from_left if step == 1 else from_right).at[g],
            near_send.at[step // 2, g],
            near_recv.at[step // 2, g],
            expert=right if step == 1 else left,
        )

    def share(g):
        pair_copy(2, far, g).wait_recv()
        mine[2, g] = joined(2, far, g).astype(jnp.bfloat16)
        go(far_copy(g))
        step, target = (1, right) if g % 2 else (3, left)
        pair_copy(step, target, g).wait_recv()
        mine[step, g] = joined(step, target, g).astype(jnp.bfloat16)
        go(near_copy(step, g))

    def add_far(g):
        step, target = (3, left) if g % 2 else (1, right)
        pair_copy(step, target, g).wait_recv()
        far_copy(g).wait_recv()
        mine[step, g] = (joined(step, target, g) + early[g].astype(jnp.float32)).astype(
            jnp.bfloat16
        )
        go(near_copy(step, g))

    def home(g, i):
        place = lax.rem(z + i, 8)
        target = group(g) * 8 + place
        return remote(
            packed.at[g, rows16(place)],
            out_ref.at[d],
            home_send.at[target],
            home_recv.at[d],
            dp=target,
        )

    home_own = pltpu.make_async_copy(packed.at[0, rows16(z)], out_ref.at[d], home_sem)

    def give(g):
        pair_copy(0, e, g).wait_recv()
        near_copy(1, g).wait_recv()
        near_copy(3, g).wait_recv()
        total = (
            joined(0, e, g) + from_left[g].astype(jnp.float32) + from_right[g].astype(jnp.float32)
        )
        packed[g] = pack_rows(packing, total.astype(jnp.bfloat16))

        def send(i, carry):
            home(g, i).start()
            return carry

        lax.fori_loop(1 if g == 0 else 0, 8, send, 0)
        if g == 0:
            home_own.start()

    outs = [
        pltpu.make_async_copy(source, target, halo_out.at[i])
        for i, (source, target) in enumerate(
            ((left_v, left_hbm), (mid_v, mid_hbm), (right_v, right_hbm))
        )
    ]

    def corner():
        for copy in halos[2:]:
            copy.wait_recv()
        for copy in corners:
            copy.start()

    def look():
        for copy in halos[:2] + corners:
            copy.wait_recv()
        for copy in outs:
            copy.start()
        bias_ref[...] = window_bias(*sizes)
        att_ref[...] = jnp.zeros_like(att_ref)
        stats_ref[...] = jnp.zeros_like(stats_ref)

    def attend(heads):
        own_rows = slice(rim, rim + tokens)
        refs = (left_v, mid_v, right_v)
        size = width // HEADS
        scale = size ** (-0.5)
        lane = lax.broadcasted_iota(jnp.int32, stats_ref.shape, 1)
        stats = stats_ref[...]
        for head in heads:
            start, low, high = head_lanes(head, size, width)
            mask = lane_mask(head, size, low, high)
            queries = mid_v[own_rows, 2 * width + low : 2 * width + high] * mask.astype(
                jnp.bfloat16
            )
            scores = nt_dot(queries, tall(refs, low, high)) * scale + bias_ref[...]
            peak = jnp.max(scores, axis=-1, keepdims=True)
            log_total = peak + jnp.log(jnp.sum(jnp.exp(scores - peak), axis=-1, keepdims=True))
            probs_low = jnp.exp(scores - log_total).astype(jnp.bfloat16)
            attended = nn_dot(probs_low, tall(refs, width + low, width + high))
            att_ref[:, low:high] += jnp.where(mask, attended, 0.0)
            stats = jnp.where(lane == head, log_total, stats)
        stats_ref[...] = stats

    def weight_grads(g):
        at = group(g)
        for lefts, rights, total, final, store in (
            (bx, grad_pre, first_acc, grad_first_v, stores[0]),
            (hidden, bg, second_acc, grad_second_v, stores[1]),
        ):
            for low in range(0, total.shape[0], 256):
                cut = slice(low, min(low + 256, total.shape[0]))
                part = tn_dot(lefts[at, :, cut], rights[at])
                if g > 0:
                    part = part + total[cut, :]
                if g < 3:
                    total[cut, :] = part
                else:
                    final[cut, :] = part.astype(jnp.bfloat16)
            if g == 3:
                store.start()

    stores = [
        pltpu.make_async_copy(grad_first_v, grad_first_hbm, store_sem.at[0]),
        pltpu.make_async_copy(grad_second_v, grad_second_hbm, store_sem.at[1]),
    ]

    arrive(0)
    arrive(1)
    relay(0)
    arrive(2)
    finish(0)
    relay(1)
    loads[2].wait()
    loads[3].wait()
    work(0)
    arrive(3)
    corner()
    finish(1)
    relay(2)
    share(0)
    work(1)
    weight_grads(0)
    finish(2)
    relay(3)
    add_far(0)
    share(1)
    work(2)
    look()
    attend(range(0, 6))
    finish(3)
    give(0)
    add_far(1)
    share(2)
    work(3)
    share(3)
    attend(range(6, 10))
    give(1)
    add_far(2)
    attend(range(10, 16))
    add_far(3)
    give(2)
    weight_grads(1)
    give(3)
    weight_grads(2)
    weight_grads(3)

    def take_home(i, carry):
        source = lax.rem(d + i, 32)
        remote(
            packed.at[0, pl.ds(0, 16)],
            out_ref.at[source],
            home_send.at[source],
            home_recv.at[source],
            dp=source,
        ).wait_recv()
        return carry

    lax.fori_loop(1, 32, take_home, 0)
    home_own.wait()
    for copy in sent + halos + corners:
        copy.wait_send()

    def sent_all(i, carry):
        message(lax.rem(d + i, 32)).wait_send()
        return carry

    lax.fori_loop(1, 32, sent_all, 0)
    for g in range(4):

        def sent_home(i, carry):
            home(g, i).wait_send()
            return carry

        lax.fori_loop(1 if g == 0 else 0, 8, sent_home, 0)
    for copy in outs + stores:
        copy.wait()


def head_lanes(head, size, width):
    start = head * size
    low = start // 128 * 128
    high = min((start + size + 127) // 128 * 128, width)
    return start, low, high


def lane_mask(head, size, low, high):
    lanes = lax.broadcasted_iota(jnp.int32, (1, high - low), 1) + low
    return (lanes >= head * size) & (lanes < (head + 1) * size)


def nt_dot(left, right):
    return lax.dot_general(left, right, (((1,), (1,)), ((), ())), preferred_element_type=jnp.float32)


def nn_dot(left, right):
    return jnp.dot(left, right, preferred_element_type=jnp.float32)


def window_bias(band, cols, rows_total, cols_total):
    row_index = lax.axis_index("dp")
    col_index = lax.axis_index("expert")
    side = (band + 2 * RAD) * cols
    shape = (band * cols, 3 * side)
    shift = cols.bit_length() - 1
    own = lax.broadcasted_iota(jnp.int32, shape, 0)
    far = lax.broadcasted_iota(jnp.int32, shape, 1)
    part = (far >= side).astype(jnp.int32) + (far >= 2 * side).astype(jnp.int32)
    within = far - side * part
    far_row = (within >> shift) - RAD
    far_col = (within & (cols - 1)) + cols * (part - 1)
    own_row = own >> shift
    own_col = own & (cols - 1)
    abs_row = far_row + row_index * band
    abs_col = far_col + col_index * cols
    fine = (
        (jnp.abs(far_row - own_row) <= RAD)
        & (jnp.abs(far_col - own_col) <= RAD)
        & (abs_row >= 0)
        & (abs_row < rows_total)
        & (abs_col >= 0)
        & (abs_col < cols_total)
    )
    return jnp.where(fine, 0.0, NEG_LARGE)


def tall(refs, low, high):
    return jnp.concatenate([ref[:, low:high] for ref in refs], axis=0)


def split_three(values):
    first = values.astype(jnp.bfloat16)
    rest = values - first.astype(jnp.float32)
    second = rest.astype(jnp.bfloat16)
    third = (rest - second.astype(jnp.float32)).astype(jnp.bfloat16)
    return first, second, third


def stream_grad(stream, grad, gain, route, back, attended, log_total):
    width = stream.shape[1]
    size = width // HEADS
    normed, inv_std, _ = layer_norm(stream, gain)
    slots = as_column(slot_numbers(route)).astype(jnp.int32)
    grad_in = unpack_rows(unpack_tables(slots, back.shape[0]), back)
    grad_stream = (
        grad.astype(jnp.float32) + norm_backward(grad_in, normed, inv_std, gain)
    ).astype(jnp.bfloat16)
    products = grad_stream.astype(jnp.float32) * attended
    feature = lax.broadcasted_iota(jnp.int32, (width, 128), 0)
    first = lax.broadcasted_iota(jnp.int32, (width, 128), 1) * size
    owner = jnp.where((feature >= first) & (feature < first + size), 1.0, 0.0).astype(jnp.bfloat16)
    delta = sum(nn_dot(piece, owner) for piece in split_three(products))
    source = lax.broadcasted_iota(jnp.int32, (128, 128), 0)
    target = lax.broadcasted_iota(jnp.int32, (128, 128), 1)
    total = jnp.zeros(delta.shape, jnp.float32)
    pieces = split_three(log_total) + split_three(delta)
    for place, piece in enumerate(pieces):
        move = (target == source + place * HEADS) & (source < HEADS)
        total = total + nn_dot(piece, jnp.where(move, 1.0, 0.0).astype(jnp.bfloat16))
    return grad_stream, total.astype(jnp.bfloat16)


def stats_table():
    row = lax.broadcasted_iota(jnp.int32, (2 * HEADS, 128), 0)
    lane = lax.broadcasted_iota(jnp.int32, (2 * HEADS, 128), 1)
    base = jnp.where(row < HEADS, row, row + 2 * HEADS)
    return jnp.where(
        (lane == base) | (lane == base + HEADS) | (lane == base + 2 * HEADS), 1.0, 0.0
    ).astype(jnp.bfloat16)


def turn_kernel(
    sizes,
    stream_hbm,
    grad_hbm,
    gain_ref,
    route_ref,
    back_ref,
    att_ref,
    stats_ref,
    left_hbm,
    mid_hbm,
    right_hbm,
    gleft_ref,
    gmid_ref,
    gright_ref,
    gq_ref,
    stream_v,
    grad_v,
    left_v,
    mid_v,
    right_v,
    query_v,
    bias_ref,
    acc_ref,
    load_sem,
    halo_send,
    halo_recv,
    corner_send,
    corner_recv,
):
    e = lax.axis_index("expert")
    d = lax.axis_index("dp")
    tokens, width = stream_hbm.shape
    size = width // HEADS
    scale = size ** (-0.5)
    rim = RAD * sizes[1]
    own = slice(rim, rim + tokens)
    both = pl.ds(0, 2 * width)
    loads = [
        pltpu.make_async_copy(source, target, load_sem.at[i])
        for i, (source, target) in enumerate(
            (
                (stream_hbm, stream_v),
                (grad_hbm, grad_v),
                (left_hbm.at[:, both], left_v),
                (mid_hbm.at[:, both], mid_v),
                (right_hbm.at[:, both], right_v),
                (mid_hbm.at[pl.ds(rim, tokens), pl.ds(2 * width, width)], query_v),
            )
        )
    ]
    for copy in loads[:2]:
        copy.start()
    barrier = pltpu.get_barrier_semaphore()
    for _, _, row, col in around(e, d):
        pl.semaphore_signal(
            barrier, inc=1, device_id={"dp": row, "expert": col}, device_id_type=MESH
        )
    loads[0].wait()
    loads[1].wait()
    for copy in loads[2:]:
        copy.start()
    plain, extra = stream_grad(
        stream_v[...],
        grad_v[...],
        gain_ref[...].reshape(1, -1),
        route_ref[...],
        back_ref[...],
        att_ref[...],
        stats_ref[...],
    )
    gmid_ref[own, :width] = plain
    gmid_ref[own, width:] = extra
    pl.semaphore_wait(barrier, 4)
    halos = []
    for number, (down, over, row, col) in enumerate(around(e, d)):
        side = {1: gleft_ref, 0: gmid_ref, -1: gright_ref}[over]
        src, dst = rim_slices(down, tokens, rim)
        src = pl.ds(src.start + rim, src.size)
        halos.append(
            remote(
                gmid_ref.at[src],
                side.at[dst],
                halo_send.at[number],
                halo_recv.at[number],
                dp=row,
                expert=col,
            )
        )
    for number in (2, 3, 0, 1):
        halos[number].start()
    corners = corner_copies(
        e, d, rim, tokens, gleft_ref, gmid_ref, gright_ref, corner_send, corner_recv
    )
    bias_ref[...] = window_bias(*sizes)
    acc_ref[...] = jnp.zeros_like(acc_ref)
    stats_own = nt_dot(gmid_ref[own, width : width + 128], stats_table())
    for copy in loads[2:]:
        copy.wait()
    refs = (left_v, mid_v, right_v)
    for head in range(HEADS):
        if head == 8:
            for copy in halos[2:]:
                copy.wait_recv()
            for copy in corners:
                copy.start()
        start, low, high = head_lanes(head, size, width)
        mask = lane_mask(head, size, low, high)
        mask_low = mask.astype(jnp.bfloat16)
        keys = tall(refs, low, high)
        values = tall(refs, width + low, width + high)
        probs = jnp.exp(
            nt_dot(query_v[:, low:high] * mask_low, keys) * scale
            + bias_ref[...]
            - stats_own[:, head : head + 1]
        )
        grad_probs = nt_dot(gmid_ref[own, low:high] * mask_low, values)
        grad_scores = (
            probs * (grad_probs - stats_own[:, HEADS + head : HEADS + head + 1])
        ).astype(jnp.bfloat16)
        acc_ref[:, low:high] += jnp.where(mask, nn_dot(grad_scores, keys), 0.0)
    gq_ref[...] = (acc_ref[...] * scale).astype(jnp.bfloat16)
    for copy in halos[:2] + corners:
        copy.wait_recv()
    for copy in halos + corners:
        copy.wait_send()


def last_kernel(
    sizes,
    left_hbm,
    mid_hbm,
    right_hbm,
    gleft_ref,
    gmid_ref,
    gright_ref,
    gq_hbm,
    first_hbm,
    second_hbm,
    gq_out,
    gk_ref,
    gv_ref,
    plain_ref,
    first_out,
    second_out,
    left_v,
    mid_v,
    right_v,
    own_v,
    bias_ref,
    acc_k,
    acc_v,
    first_v,
    second_v,
    gq_v,
    load_sem,
    pass_sem,
):
    tokens, width = gk_ref.shape
    size = width // HEADS
    scale = size ** (-0.5)
    rim = RAD * sizes[1]
    own = slice(rim, rim + tokens)
    third = pl.ds(2 * width, width)
    loads = [
        pltpu.make_async_copy(source, target, load_sem.at[i])
        for i, (source, target) in enumerate(
            (
                (left_hbm.at[:, third], left_v),
                (mid_hbm.at[:, third], mid_v),
                (right_hbm.at[:, third], right_v),
                (mid_hbm.at[pl.ds(rim, tokens), pl.ds(0, 2 * width)], own_v),
            )
        )
    ]
    fetched = [
        pltpu.make_async_copy(source, target, pass_sem.at[i])
        for i, (source, target) in enumerate(
            ((first_hbm, first_v), (second_hbm, second_v), (gq_hbm, gq_v))
        )
    ]
    passed = [
        pltpu.make_async_copy(source, target, pass_sem.at[i])
        for i, (source, target) in enumerate(
            ((first_v, first_out), (second_v, second_out), (gq_v, gq_out))
        )
    ]
    for copy in loads:
        copy.start()
    plain_ref[...] = gmid_ref[own, :width]
    bias_ref[...] = window_bias(*sizes)
    acc_k[...] = jnp.zeros_like(acc_k)
    acc_v[...] = jnp.zeros_like(acc_v)
    refs = (left_v, mid_v, right_v)
    grefs = (gleft_ref, gmid_ref, gright_ref)
    stats_far = nt_dot(stats_table(), tall(grefs, width, width + 128))
    for copy in loads:
        copy.wait()
    for head in range(HEADS):
        if head == 0:
            for copy in fetched:
                copy.start()
        if head == 8:
            for before, after in zip(fetched, passed):
                before.wait()
                after.start()
        start, low, high = head_lanes(head, size, width)
        mask = lane_mask(head, size, low, high)
        mask_low = mask.astype(jnp.bfloat16)
        queries = tall(refs, low, high)
        grads = tall(grefs, low, high)
        probs = jnp.exp(
            nt_dot(own_v[:, low:high] * mask_low, queries) * scale
            + bias_ref[...]
            - stats_far[head : head + 1, :]
        )
        acc_v[:, low:high] += jnp.where(mask, nn_dot(probs.astype(jnp.bfloat16), grads), 0.0)
        grad_probs = nt_dot(own_v[:, width + low : width + high] * mask_low, grads)
        grad_scores = (
            probs * (grad_probs - stats_far[HEADS + head : HEADS + head + 1, :])
        ).astype(jnp.bfloat16)
        acc_k[:, low:high] += jnp.where(mask, nn_dot(grad_scores, queries), 0.0)
    gk_ref[...] = (acc_k[...] * scale).astype(jnp.bfloat16)
    gv_ref[...] = acc_v[...].astype(jnp.bfloat16)
    for copy in passed:
        copy.wait()


def vmem():
    return pl.BlockSpec(memory_space=pltpu.VMEM)


def anywhere():
    return pl.BlockSpec(memory_space=pl.ANY)


def params(collective_id):
    limit = VMEM_LIMIT if collective_id == 1 else TAIL_LIMIT
    return pltpu.CompilerParams(
        vmem_limit_bytes=limit, collective_id=collective_id, has_side_effects=True
    )


def shaped(shape, kind=jnp.bfloat16):
    return jax.ShapeDtypeStruct(shape, kind)


def body(
    query_act,
    key_act,
    value_act,
    stream,
    grad_out,
    norm_gain,
    route_ids,
    gate_prob,
    weight_in,
    weight_out,
):
    band, cols, width = stream.shape
    tokens = band * cols
    experts = lax.axis_size("dp")
    col_parts = lax.axis_size("expert")
    sizes = (band, cols, band * experts, cols * col_parts)
    side = (band + 2 * RAD) * cols
    dma = pltpu.SemaphoreType.DMA
    flat_query, flat_key, flat_value, flat_stream, flat_grad = (
        array.reshape(tokens, width) for array in (query_act, key_act, value_act, stream, grad_out)
    )
    gain = norm_gain
    routes = route_ids.reshape(1, tokens)
    bf = jnp.bfloat16
    hidden_units = weight_in.shape[-1]
    *near, returned, attended, log_total, grad_first, grad_second = pl.pallas_call(
        functools.partial(expert_kernel, sizes),
        out_shape=(shaped((side, 3 * width)),) * 3
        + (
            shaped((experts, 16, 640)),
            shaped((tokens, width), jnp.float32),
            shaped((tokens, 128), jnp.float32),
            shaped((width, hidden_units)),
            shaped((hidden_units, width)),
        ),
        in_specs=[anywhere()] * 2 + [vmem()] * 3 + [anywhere()] * 5,
        out_specs=(anywhere(),) * 3 + (vmem(),) * 3 + (anywhere(),) * 2,
        scratch_shapes=[
            pltpu.VMEM((tokens, width), bf),
            pltpu.VMEM((tokens, width), bf),
            pltpu.VMEM((width, hidden_units), bf),
            pltpu.VMEM((hidden_units, width), bf),
            pltpu.VMEM((experts * 16, 1280), bf),
            pltpu.VMEM((4, 128, 1280), bf),
            pltpu.VMEM((4, 384, width), bf),
            pltpu.VMEM((4, 384, width), bf),
            pltpu.VMEM((4, 384, hidden_units), bf),
            pltpu.VMEM((4, 384, hidden_units), bf),
            pltpu.VMEM((4, 384, width), bf),
            pltpu.VMEM((4, 4, 48, width), bf),
            pltpu.VMEM((4, 4, 48, width), bf),
            pltpu.VMEM((4, 48, width), bf),
            pltpu.VMEM((4, 48, width), bf),
            pltpu.VMEM((4, 48, width), bf),
            pltpu.VMEM((4, 128, 640), bf),
            pltpu.VMEM((side, 3 * width), bf),
            pltpu.VMEM((side, 3 * width), bf),
            pltpu.VMEM((side, 3 * width), bf),
            pltpu.VMEM((tokens, 3 * side), jnp.float32),
            pltpu.VMEM((width, hidden_units), bf),
            pltpu.VMEM((hidden_units, width), bf),
            pltpu.VMEM((width, hidden_units), jnp.float32),
            pltpu.VMEM((hidden_units, width), jnp.float32),
            dma((4,)),
            dma((2,)),
            dma((4,)),
            dma((4,)),
            dma((3,)),
            dma((3,)),
            dma((4,)),
            dma((4,)),
            dma((32,)),
            dma((32,)),
            dma,
            dma((4, 2, 7)),
            dma((8, 4, 2)),
            dma((4, 4)),
            dma((4, 4)),
            dma((4,)),
            dma((4,)),
            dma((2, 4)),
            dma((2, 4)),
            dma((32,)),
            dma((32,)),
            dma,
        ],
        compiler_params=params(1),
        name="expert",
    )(
        flat_stream,
        flat_grad,
        gain,
        gate_prob.reshape(1, tokens),
        routes,
        flat_key,
        flat_value,
        flat_query,
        weight_in[0],
        weight_out[0],
    )
    gleft, gmid, gright, grad_query = pl.pallas_call(
        functools.partial(turn_kernel, sizes),
        out_shape=(shaped((side, width + 128)),) * 3 + (shaped((tokens, width)),),
        in_specs=[anywhere()] * 2 + [vmem()] * 5 + [anywhere()] * 3,
        out_specs=(vmem(),) * 4,
        scratch_shapes=[
            pltpu.VMEM((tokens, width), bf),
            pltpu.VMEM((tokens, width), bf),
            pltpu.VMEM((side, 2 * width), bf),
            pltpu.VMEM((side, 2 * width), bf),
            pltpu.VMEM((side, 2 * width), bf),
            pltpu.VMEM((tokens, width), bf),
            pltpu.VMEM((tokens, 3 * side), jnp.float32),
            pltpu.VMEM((tokens, width), jnp.float32),
            dma((6,)),
            dma((4,)),
            dma((4,)),
            dma((4,)),
            dma((4,)),
        ],
        compiler_params=params(2),
        name="turn",
    )(
        flat_stream,
        flat_grad,
        gain,
        routes,
        returned.reshape(-1, 640),
        attended,
        log_total,
        *near,
    )
    grad_query, grad_key, grad_value, plain, grad_first, grad_second = pl.pallas_call(
        functools.partial(last_kernel, sizes),
        out_shape=(shaped((tokens, width)),) * 4
        + (shaped((width, hidden_units)), shaped((hidden_units, width))),
        in_specs=[anywhere()] * 3 + [vmem()] * 3 + [anywhere()] * 3,
        out_specs=(anywhere(),) + (vmem(),) * 3 + (anywhere(),) * 2,
        scratch_shapes=[
            pltpu.VMEM((side, width), bf),
            pltpu.VMEM((side, width), bf),
            pltpu.VMEM((side, width), bf),
            pltpu.VMEM((tokens, 2 * width), bf),
            pltpu.VMEM((tokens, 3 * side), jnp.float32),
            pltpu.VMEM((tokens, width), jnp.float32),
            pltpu.VMEM((tokens, width), jnp.float32),
            pltpu.VMEM((width, hidden_units), bf),
            pltpu.VMEM((hidden_units, width), bf),
            pltpu.VMEM((tokens, width), bf),
            dma((4,)),
            dma((3,)),
        ],
        compiler_params=pltpu.CompilerParams(vmem_limit_bytes=TAIL_LIMIT),
        name="last",
    )(*near, gleft, gmid, gright, grad_query, grad_first, grad_second)
    shape = (band, cols, width)
    return (
        grad_query.reshape(shape),
        grad_key.reshape(shape),
        grad_value.reshape(shape),
        plain.reshape(shape),
        grad_first[None],
        grad_second[None],
    )


def solution(mesh):
    in_specs = (
        P("dp", "expert", None),
        P("dp", "expert", None),
        P("dp", "expert", None),
        P("dp", "expert", None),
        P("dp", "expert", None),
        P(),
        P("dp", "expert", None, None),
        P("dp", "expert", None),
        P("dp", None, "expert"),
        P("dp", "expert", None),
    )
    out_specs = (
        P("dp", "expert", None),
        P("dp", "expert", None),
        P("dp", "expert", None),
        P("dp", "expert", None),
        P("dp", None, "expert"),
        P("dp", "expert", None),
    )
    return jax.shard_map(body, mesh=mesh, in_specs=in_specs, out_specs=out_specs, check_vma=False)
```
